128 devices in a mesh: ctx: 8 (over y, x_hi), head: 16 (over x_lo, z, core).
Axes of the slice: x: 4 (x_hi: 2, x_lo: 2; x = x_hi * 2 + x_lo), y: 4, z: 4, core: 2. Of those that a mesh axis runs over, the one named last changes fastest.
Arguments:
- query: bfloat16 [16384, 32, 128], P(('ctx', 'head')), may hold values from -6 to 6
- keys: bfloat16 [16384, 32, 128], P(('ctx', 'head')), may hold values from -6 to 6
- values: bfloat16 [16384, 32, 128], P(('ctx', 'head')), may hold values from -6 to 6
- grad_out: bfloat16 [16384, 32, 128], P(('ctx', 'head')), may hold values from -6 to 6
- window: int32 [32], P('head'), may hold values from 1 to 8, as said below
- global_blocks: int32 [6], replicated, may hold values from 0 to 127, as said below
Outputs:
- attended: bfloat16 [16384, 32, 128], P(('ctx', 'head'))
- grad_query: bfloat16 [16384, 32, 128], P(('ctx', 'head'))
- grad_keys: bfloat16 [16384, 32, 128], P(('ctx', 'head'))
- grad_values: bfloat16 [16384, 32, 128], P(('ctx', 'head'))
The draws below stay inside these ranges and needn't reach their ends.
Inputs may be any that keep to these rules, and one draw needn't show every extreme that they name: Some head has a window of exactly 8 blocks. `global_blocks`: 6 distinct block indices; blocks 0 and 127 are always among them.
All inputs are finite; a program needn't handle non-finite values.
Results may differ from the reference program's by a relative error of at most 0.019.
Values may be sent and summed in bfloat16 or wider, within the bound.
No kernel may reach another device: no remote copies, remote signals or barrier semaphores. Data moves between devices by JAX's collectives and lax.ppermute only.
A program may use at most 128 MiB of HBM per device.

```python
import jax
import jax.numpy as jnp
from jax import lax

HD = 128
BLK = 128
GLOB = 6
SEG = 1024
WIN = 8
SEQ = 16384
NBLK = 128
HEADS = 32
N_CTX = 8


def base_field(key):
    return jnp.clip(jax.random.normal(key, (SEQ, HEADS, HD), jnp.float32), -6.0, 6.0)


def draw_query(key, part):
    field = base_field(jax.random.fold_in(key, 1))
    return field.astype(jnp.bfloat16)


def draw_keys(key, part):
    field = base_field(jax.random.fold_in(key, 2))
    return field.astype(jnp.bfloat16)


def draw_window(key, part):
    base = jax.random.randint(jax.random.fold_in(key, 11), (HEADS,), 1, WIN + 1)
    chosen = jax.random.randint(jax.random.fold_in(key, 12), (), 0, HEADS)
    return jnp.where(jnp.arange(HEADS) == chosen, WIN, base).astype(jnp.int32)


def draw_global_blocks(key, part):
    middle = jax.random.permutation(jax.random.fold_in(key, 21), NBLK - 2)[:GLOB - 2] + 1
    first = jnp.zeros((1,), jnp.int32)
    final = jnp.full((1,), NBLK - 1, jnp.int32)
    return jnp.concatenate([first, middle.astype(jnp.int32), final]).astype(jnp.int32)


def steps_of(key, dims, cuts, least, high):
    level = 1.0
    for position, blocks in cuts:
        heights = jax.random.uniform(jax.random.fold_in(jax.random.fold_in(key, 6), position), (blocks,), jnp.float32, least / len(cuts), high / len(cuts))
        level = level * jnp.repeat(jnp.exp(heights), dims[position] // blocks).reshape((-1,) + (1,) * (len(dims) - 1 - position))
    return level


def gaussian(rng, dims, scale, bound, shards=(), kind=jnp.bfloat16):
    entries = scale * jax.random.normal(rng, dims, jnp.float32)
    if shards:
        entries = entries * steps_of(rng, dims, shards, -0.22, 0.18)
    return jnp.clip(entries, -bound, bound).astype(kind)


def setup_inputs(seed: int = 0) -> dict:
    seeds = jax.random.split(jax.random.key(seed), 7)
    return {
        "query": draw_query(jax.random.fold_in(seeds[6], 71), 0),
        "keys": draw_keys(jax.random.fold_in(seeds[6], 71), 0),
        "values": gaussian(seeds[2], (SEQ, HEADS, HD), 1.0, 6.0, ((0, 128),)),
        "grad_out": gaussian(seeds[3], (SEQ, HEADS, HD), 1.0, 6.0, ((0, 128),)),
        "window": draw_window(jax.random.fold_in(seeds[6], 71), 0),
        "global_blocks": draw_global_blocks(jax.random.fold_in(seeds[6], 71), 0),
    }


NEG_FILL = -1.0e30


def rounded(source):
    return lax.optimization_barrier(source.astype(jnp.bfloat16)).astype(jnp.float32)


def to_sequence(stored):
    parts = stored.reshape((N_CTX, 2, SEG) + stored.shape[1:])
    return jnp.concatenate([parts[:, 0], parts[::-1, 1]], axis=0).reshape(stored.shape)


def to_stored(ordered):
    parts = ordered.reshape((2 * N_CTX, SEG) + ordered.shape[1:])
    return jnp.stack([parts[:N_CTX], parts[N_CTX:][::-1]], axis=1).reshape(ordered.shape)


def head_pass(query, keys, values, grad_out, width, global_blocks):
    count = SEQ // SEG
    scale = HD ** -0.5
    query_seg = query.reshape(count, SEG, HD).astype(jnp.float32)
    grad_seg = grad_out.reshape(count, SEG, HD).astype(jnp.float32)
    key_seg = keys.reshape(count, SEG, HD).astype(jnp.float32)
    value_seg = values.reshape(count, SEG, HD).astype(jnp.float32)
    empty = jnp.zeros((1, SEG, HD), jnp.float32)
    band_keys = jnp.concatenate([jnp.concatenate([empty, key_seg[:-1]], axis=0), key_seg], axis=1)
    band_values = jnp.concatenate([jnp.concatenate([empty, value_seg[:-1]], axis=0), value_seg], axis=1)
    glob_rows = (global_blocks[:, None] * BLK + jnp.arange(BLK, dtype=jnp.int32)[None, :]).reshape(-1)
    glob_keys = keys[glob_rows].astype(jnp.float32)
    glob_values = values[glob_rows].astype(jnp.float32)
    glob_cols = jnp.repeat(global_blocks, BLK)
    query_pos = jnp.arange(SEQ, dtype=jnp.int32).reshape(count, SEG)
    key_pos = query_pos[:, :1] - SEG + jnp.arange(2 * SEG, dtype=jnp.int32)[None, :]
    query_blk = query_pos // BLK
    band_ok = (key_pos[:, None, :] >= 0) & (key_pos[:, None, :] <= query_pos[:, :, None]) & (query_blk[:, :, None] - key_pos[:, None, :] // BLK < width)
    glob_ok = glob_cols[None, None, :] <= query_blk[:, :, None] - width
    band_s = jnp.where(band_ok, jnp.einsum("cqd,ckd->cqk", query_seg, band_keys) * scale, NEG_FILL)
    glob_s = jnp.where(glob_ok, jnp.einsum("cqd,kd->cqk", query_seg, glob_keys) * scale, NEG_FILL)
    top = jnp.maximum(jnp.max(band_s, axis=2), jnp.max(glob_s, axis=2))
    total = jnp.sum(jnp.exp(band_s - top[..., None]), axis=2) + jnp.sum(jnp.exp(glob_s - top[..., None]), axis=2)
    log_total = top + jnp.log(total)
    band_p = jnp.exp(band_s - log_total[..., None])
    glob_p = jnp.exp(glob_s - log_total[..., None])
    band_w = rounded(band_p)
    glob_w = rounded(glob_p)
    attended = (jnp.einsum("cqk,ckd->cqd", band_w, band_values) + jnp.einsum("cqk,kd->cqd", glob_w, glob_values)).astype(jnp.bfloat16)
    delta = jnp.sum(grad_seg * attended.astype(jnp.float32), axis=2)
    band_ds = rounded(band_p * (jnp.einsum("cqd,ckd->cqk", grad_seg, band_values) - delta[..., None]))
    glob_ds = rounded(glob_p * (jnp.einsum("cqd,kd->cqk", grad_seg, glob_values) - delta[..., None]))
    grad_query = (jnp.einsum("cqk,ckd->cqd", band_ds, band_keys) + jnp.einsum("cqk,kd->cqd", glob_ds, glob_keys)) * scale
    band_dk = jnp.einsum("cqk,cqd->ckd", band_ds, query_seg) * scale
    band_dv = jnp.einsum("cqk,cqd->ckd", band_w, grad_seg)
    tail = jnp.zeros((1, SEG, HD), jnp.float32)
    grad_keys = (band_dk[:, SEG:] + jnp.concatenate([band_dk[1:, :SEG], tail], axis=0)).reshape(SEQ, HD)
    grad_values = (band_dv[:, SEG:] + jnp.concatenate([band_dv[1:, :SEG], tail], axis=0)).reshape(SEQ, HD)
    grad_keys = grad_keys.at[glob_rows].add(jnp.einsum("cqk,cqd->kd", glob_ds, query_seg) * scale)
    grad_values = grad_values.at[glob_rows].add(jnp.einsum("cqk,cqd->kd", glob_w, grad_seg))
    return (attended.reshape(SEQ, HD), grad_query.reshape(SEQ, HD).astype(jnp.bfloat16), grad_keys.astype(jnp.bfloat16), grad_values.astype(jnp.bfloat16))


def reference(query, keys, values, grad_out, window, global_blocks):
    query_h = jnp.moveaxis(to_sequence(query), 1, 0)
    keys_h = jnp.moveaxis(to_sequence(keys), 1, 0)
    values_h = jnp.moveaxis(to_sequence(values), 1, 0)
    grad_h = jnp.moveaxis(to_sequence(grad_out), 1, 0)

    def one_head(inputs):
        return head_pass(inputs[0], inputs[1], inputs[2], inputs[3], inputs[4], global_blocks)

    attended, grad_query, grad_keys, grad_values = lax.map(one_head, (query_h, keys_h, values_h, grad_h, window))
    return (to_stored(jnp.moveaxis(attended, 0, 1)), to_stored(jnp.moveaxis(grad_query, 0, 1)), to_stored(jnp.moveaxis(grad_keys, 0, 1)), to_stored(jnp.moveaxis(grad_values, 0, 1)))
```

```python
import functools

import jax
import jax.numpy as jnp
from jax import lax
from jax.experimental import pallas as pl
from jax.experimental.pallas import tpu as pltpu
from jax.sharding import Mesh, PartitionSpec as P

BLK = 128
HD = 128
WIN = 8
HALO = WIN - 1
RUN = 16
EXT = HALO + RUN
GLOB = 6
BAND = WIN + 1
NEG = -1e30
SCALE = HD ** -0.5
LOG2E = 1.4426950408889634
GROUP = ("xh", "xl", "z", "c")
F32 = jnp.float32
BF16 = jnp.bfloat16


def dot(a, b):
    return jnp.dot(a, b, preferred_element_type=F32)


def attention_kernel(
    info, kv, qd, halo_a, halo_b, glob,
    odq, own, back_a, back_b, glob_grad,
    kx, vx, kt, vt, kgt, vgt, dk, dv, dkg, dvg, st, pb, ds,
):
    w = info[0]
    last_y = info[1]
    for h in range(HALO):
        kx[0, h] = halo_a[h, 0]
        vx[0, h] = halo_a[h, 1]
        kx[1, h] = halo_b[h, 0]
        vx[1, h] = halo_b[h, 1]

    @pl.when(last_y == 1)
    def _():
        for h in range(HALO):
            kx[1, h] = kv[17 + h, 0]
            vx[1, h] = kv[17 + h, 1]

    for t in range(RUN):
        p0 = (t // 8) * 16 + t % 8
        p1 = (1 - t // 8) * 16 + 8 + t % 8
        kx[0, HALO + t] = kv[p0, 0]
        vx[0, HALO + t] = kv[p0, 1]
        kx[1, HALO + t] = kv[p1, 0]
        vx[1, HALO + t] = kv[p1, 1]
    for e in range(EXT):
        for ch in range(2):
            kt[ch, :, e * BLK:(e + 1) * BLK] = kx[ch, e].T
            vt[ch, :, e * BLK:(e + 1) * BLK] = vx[ch, e].T
    for s in range(GLOB):
        kgt[:, s * BLK:(s + 1) * BLK] = glob[s, 0].T
        vgt[:, s * BLK:(s + 1) * BLK] = glob[s, 1].T
    dk[...] = jnp.zeros_like(dk)
    dv[...] = jnp.zeros_like(dv)
    dkg[...] = jnp.zeros_like(dkg)
    dvg[...] = jnp.zeros_like(dvg)

    lane = lax.broadcasted_iota(jnp.int32, (1, 2 * BLK), 1)
    upper = lane // BLK
    lane_full = lax.broadcasted_iota(jnp.int32, (BLK, 2 * BLK), 1)
    row_full = lax.broadcasted_iota(jnp.int32, (BLK, 2 * BLK), 0)
    c = SCALE * LOG2E

    def tile(ch, tt):
        t0 = 2 * tt
        seg = tt // 4
        if ch == 0:
            pos = seg * 16 + t0 - seg * 8
        else:
            pos = (1 - seg) * 16 + 8 + t0 - seg * 8
        base = info[2 + ch]
        first = base + t0
        q = qd[pl.ds(pos, 2), 0].reshape(2 * BLK, HD)
        do = qd[pl.ds(pos, 2), 1].reshape(2 * BLK, HD)
        qt = q.T
        dot_ = do.T
        top = None
        for r in range(BAND):
            s = dot(kx[ch, t0 + r], qt)
            if r >= BAND - 2:
                s = jnp.where(row_full <= lane_full - BLK * (r - HALO), s, NEG)
            dist = HALO - r + upper
            ok = jnp.logical_and(dist < w, first - HALO + r >= 0)
            s = jnp.where(ok, s, NEG)
            st[r * BLK:(r + 1) * BLK] = s
            here = jnp.max(s.reshape(BLK // 8, 8, 2 * BLK), axis=0)
            top = here if top is None else jnp.maximum(top, here)
        for g in range(GLOB):
            s = dot(glob[g, 0], qt)
            ok = info[4 + g] <= first + upper - w
            s = jnp.where(ok, s, NEG)
            st[(BAND + g) * BLK:(BAND + g + 1) * BLK] = s
            top = jnp.maximum(top, jnp.max(s.reshape(BLK // 8, 8, 2 * BLK), axis=0))
        top = jnp.max(top, axis=0, keepdims=True) * c
        total = None
        for r in range(BAND + GLOB):
            rows = slice(r * BLK, (r + 1) * BLK)
            e = jnp.exp2(st[rows] * c - top)
            st[rows] = e
            here = jnp.sum(e.reshape(BLK // 8, 8, 2 * BLK), axis=0)
            total = here if total is None else total + here
        inv = 1.0 / jnp.sum(total, axis=0, keepdims=True)
        for r in range(BAND + GLOB):
            rows = slice(r * BLK, (r + 1) * BLK)
            e = st[rows] * inv
            st[rows] = e
            pb[rows] = e.astype(BF16)
        cut = BAND * BLK
        cols = pl.ds(pl.multiple_of(t0 * BLK, 2 * BLK), cut)
        ot = dot(vt[ch, :, cols], pb[:cut]) + dot(vgt[...], pb[cut:])
        ob = ot.astype(BF16)
        delta = jnp.sum(ob.astype(F32) * dot_.astype(F32), axis=0, keepdims=True)
        odq[pl.ds(pos, 2), 0] = ob.T.reshape(2, BLK, HD)
        for r in range(BAND + GLOB):
            rows = slice(r * BLK, (r + 1) * BLK)
            v = vx[ch, t0 + r] if r < BAND else glob[r - BAND, 1]
            g = (st[rows] * (dot(v, dot_) - delta)).astype(BF16)
            ds[rows] = g
            if r < BAND:
                dk[ch, t0 + r] += dot(g, q)
                dv[ch, t0 + r] += dot(pb[rows], do)
            else:
                dkg[r - BAND] += dot(g, q)
                dvg[r - BAND] += dot(pb[rows], do)
        dqt = (dot(kt[ch, :, cols], ds[:cut]) + dot(kgt[...], ds[cut:])) * SCALE
        odq[pl.ds(pos, 2), 1] = dqt.astype(BF16).T.reshape(2, BLK, HD)

    def step(tt, carry):
        tile(0, tt)
        tile(1, tt)
        return carry

    lax.fori_loop(0, RUN // 2, step, 0)

    for t in range(RUN):
        p0 = (t // 8) * 16 + t % 8
        p1 = (1 - t // 8) * 16 + 8 + t % 8
        own[p0, 0] = dk[0, HALO + t] * SCALE
        own[p0, 1] = dv[0, HALO + t]
        own[p1, 0] = dk[1, HALO + t] * SCALE
        own[p1, 1] = dv[1, HALO + t]

    @pl.when(last_y == 1)
    def _():
        for h in range(HALO):
            own[17 + h, 0] += dk[1, h] * SCALE
            own[17 + h, 1] += dv[1, h]

    for h in range(HALO):
        back_a[h, 0] = (dk[0, h] * SCALE).astype(BF16)
        back_a[h, 1] = dv[0, h].astype(BF16)
        back_b[h, 0] = (dk[1, h] * SCALE).astype(BF16)
        back_b[h, 1] = dv[1, h].astype(BF16)
    for g in range(GLOB):
        glob_grad[g, 0] = (dkg[g] * SCALE).astype(BF16)
        glob_grad[g, 1] = dvg[g].astype(BF16)


def vmem():
    return pl.BlockSpec(memory_space=pltpu.VMEM)


def attention(info, kv, qd, halo_a, halo_b, glob):
    sds = jax.ShapeDtypeStruct
    return pl.pallas_call(
        attention_kernel,
        out_shape=(
            sds((32, 2, BLK, HD), BF16),
            sds((32, 2, BLK, HD), F32),
            sds((HALO, 2, BLK, HD), BF16),
            sds((HALO, 2, BLK, HD), BF16),
            sds((GLOB, 2, BLK, HD), BF16),
        ),
        in_specs=[pl.BlockSpec(memory_space=pltpu.SMEM)] + [vmem()] * 5,
        out_specs=(vmem(),) * 5,
        scratch_shapes=[
            pltpu.VMEM((2, EXT, BLK, HD), BF16),
            pltpu.VMEM((2, EXT, BLK, HD), BF16),
            pltpu.VMEM((2, HD, EXT * BLK + BLK), BF16),
            pltpu.VMEM((2, HD, EXT * BLK + BLK), BF16),
            pltpu.VMEM((HD, GLOB * BLK), BF16),
            pltpu.VMEM((HD, GLOB * BLK), BF16),
            pltpu.VMEM((2, EXT, BLK, HD), F32),
            pltpu.VMEM((2, EXT, BLK, HD), F32),
            pltpu.VMEM((GLOB, BLK, HD), F32),
            pltpu.VMEM((GLOB, BLK, HD), F32),
            pltpu.VMEM(((BAND + GLOB) * BLK, 2 * BLK), F32),
            pltpu.VMEM(((BAND + GLOB) * BLK, 2 * BLK), BF16),
            pltpu.VMEM(((BAND + GLOB) * BLK, 2 * BLK), BF16),
        ],
        compiler_params=pltpu.CompilerParams(vmem_limit_bytes=52 * 2**20),
        cost_estimate=pl.CostEstimate(
            flops=12 * 448 * BLK**3, bytes_accessed=16 * 2**20, transcendentals=448 * BLK * BLK
        ),
        name="attention",
    )(info, kv, qd, halo_a, halo_b, glob)


def finish_kernel(info, own, back_a, back_b, glob_one, glob_two, out):
    for p in range(32):
        for a in range(2):
            g = own[p, a]
            if 17 <= p < 24:
                g = g + back_a[p - 17, a].astype(F32)
            if 9 <= p < 16:
                g = g + back_b[p - 9, a].astype(F32)
            own_p = g
            out[p, a] = own_p.astype(BF16)
    for s in range(GLOB):
        @pl.when(info[16 + s] == 1)
        def _(s=s):
            p = info[10 + s]
            for a in range(2):
                g = own[p, a] + glob_one[s, a].astype(F32) + glob_two[s, a].astype(F32)
                ia = jnp.clip(p - 17, 0, HALO - 1)
                ib = jnp.clip(p - 9, 0, HALO - 1)
                in_a = jnp.logical_and(p >= 17, p < 24)
                in_b = jnp.logical_and(p >= 9, p < 16)
                g = g + jnp.where(in_a, back_a[ia, a].astype(F32), 0.0)
                g = g + jnp.where(in_b, back_b[ib, a].astype(F32), 0.0)
                out[p, a] = g.astype(BF16)


def finish(info, own, back_a, back_b, glob_one, glob_two):
    return pl.pallas_call(
        finish_kernel,
        out_shape=jax.ShapeDtypeStruct((32, 2, BLK, HD), BF16),
        in_specs=[pl.BlockSpec(memory_space=pltpu.SMEM)] + [vmem()] * 5,
        out_specs=vmem(),
        compiler_params=pltpu.CompilerParams(vmem_limit_bytes=24 * 2**20),
        cost_estimate=pl.CostEstimate(flops=2**21, bytes_accessed=8 * 2**20, transcendentals=0),
        name="finish",
    )(info, own, back_a, back_b, glob_one, glob_two)


def to_heads(x, y):
    pair = jnp.stack([x, y], axis=0).reshape(2, BLK, 16, 2, HD)
    pair = jnp.transpose(pair, (3, 2, 0, 1, 4)).reshape(32, 2, BLK, HD)
    return pair


def to_rows(pair):
    pair = pair.reshape(2, 16, 2, BLK, HD)
    pair = jnp.transpose(pair, (2, 3, 1, 0, 4)).reshape(2, BLK, 32, HD)
    return pair[0], pair[1]


def exchange(x):
    return lax.all_to_all(x, GROUP, 0, 0, tiled=True)


PAIR_ONE = [(0, 1), (1, 0), (2, 3), (3, 2)]
PAIR_TWO = [(1, 2), (2, 1), (3, 0), (0, 3)]


def shards(query, keys, values, grad_out, window, global_blocks):
    me = lax.axis_index("y")
    w = jnp.where(lax.axis_index("xh") == 0, window[0], window[1])
    low = global_blocks < 64
    owner = jnp.where(low, global_blocks // RUN, (127 - global_blocks) // RUN)
    t = global_blocks % RUN
    where = jnp.where(low, (t // 8) * 16 + t % 8, (1 - t // 8) * 16 + 8 + t % 8)
    info = jnp.concatenate([
        jnp.stack([w, (me == 3).astype(jnp.int32), RUN * me, 112 - RUN * me]),
        global_blocks, where, (owner == me).astype(jnp.int32),
    ]).astype(jnp.int32)

    kv = exchange(to_heads(keys, values))
    qd = exchange(to_heads(query, grad_out))

    halo_a = lax.ppermute(kv[17:24], "y", [(0, 1), (1, 2), (2, 3)])
    halo_b = lax.ppermute(kv[9:16], "y", [(3, 2), (2, 1), (1, 0)])
    mine = jnp.concatenate([lax.dynamic_slice_in_dim(kv, where[s], 1, 0) for s in range(GLOB)], axis=0)
    other = lax.ppermute(mine, "y", PAIR_ONE)
    mine = jnp.where((owner == me)[:, None, None, None], mine, other)
    other = lax.ppermute(mine, "y", PAIR_TWO)
    glob = jnp.where((owner // 2 == me // 2)[:, None, None, None], mine, other)

    odq, own, back_a, back_b, glob_grad = attention(info, kv, qd, halo_a, halo_b, glob)

    odq = exchange(odq)
    back_a = lax.ppermute(back_a, "y", [(1, 0), (2, 1), (3, 2)])
    back_b = lax.ppermute(back_b, "y", [(0, 1), (1, 2), (2, 3)])
    other = lax.ppermute(glob_grad, "y", PAIR_ONE)
    glob_grad = (glob_grad.astype(F32) + other.astype(F32)).astype(BF16)
    other = lax.ppermute(glob_grad, "y", PAIR_TWO)
    dkv = exchange(finish(info, own, back_a, back_b, glob_grad, other))
    attended, grad_query = to_rows(odq)
    grad_keys, grad_values = to_rows(dkv)
    return attended, grad_query, grad_keys, grad_values


def solution(mesh):
    fine = Mesh(mesh.devices.reshape(4, 2, 2, 4, 2), ("y", "xh", "xl", "z", "c"))
    rows = P(("y", "xh", "xl", "z", "c"), None, None)
    return jax.shard_map(
        shards,
        mesh=fine,
        in_specs=(rows, rows, rows, rows, P(("xl", "z", "c")), P()),
        out_specs=(rows,) * 4,
        check_vma=False,
    )
```

```python
import functools

import jax
import jax.numpy as jnp
from jax import lax
from jax.experimental import pallas as pl
from jax.experimental.pallas import tpu as pltpu
from jax.sharding import Mesh, PartitionSpec as P

BLK = 128
HD = 128
WIN = 8
HALO = WIN - 1
RUN = 16
EXT = HALO + RUN
GLOB = 6
BAND = WIN + 1
NEG = -1e30
SCALE = HD ** -0.5
LOG2E = 1.4426950408889634
GROUP = ("xh", "xl", "z", "c")
F32 = jnp.float32
BF16 = jnp.bfloat16


def dot(a, b):
    return jnp.dot(a, b, preferred_element_type=F32)


def attention_kernel(
    info, kv, qd, halo_a, halo_b, glob,
    odq, own, back_a, back_b, glob_grad,
    kx, vx, kt, vt, kgt, vgt, qs, dos, st, pb, ds, pg, dg, dkg, dvg, tail,
):
    w = info[0]
    last_y = info[1]
    for h in range(HALO):
        kx[0, h] = halo_a[h, 0]
        vx[0, h] = halo_a[h, 1]
        kx[1, h] = halo_b[h, 0]
        vx[1, h] = halo_b[h, 1]

    @pl.when(last_y == 1)
    def _():
        for h in range(HALO):
            kx[1, h] = kv[17 + h, 0]
            vx[1, h] = kv[17 + h, 1]

    for t in range(RUN):
        for ch in range(2):
            p = place(ch, t)
            kx[ch, HALO + t] = kv[p, 0]
            vx[ch, HALO + t] = kv[p, 1]
    for e in range(EXT):
        for ch in range(2):
            kt[ch, :, e * BLK:(e + 1) * BLK] = kx[ch, e].T
            vt[ch, :, e * BLK:(e + 1) * BLK] = vx[ch, e].T
    for s in range(GLOB):
        kgt[:, s * BLK:(s + 1) * BLK] = glob[s, 0].T
        vgt[:, s * BLK:(s + 1) * BLK] = glob[s, 1].T

    upper = lax.broadcasted_iota(jnp.int32, (1, 2 * BLK), 1) // BLK
    lane_full = lax.broadcasted_iota(jnp.int32, (BLK, 2 * BLK), 1)
    row_full = lax.broadcasted_iota(jnp.int32, (BLK, 2 * BLK), 0)
    c = SCALE * LOG2E
    cut = BAND * BLK

    def tile(ch, tt, slot):
        t0 = 2 * tt
        seg = tt // 4
        if ch == 0:
            pos = seg * 16 + t0 - seg * 8
        else:
            pos = (1 - seg) * 16 + 8 + t0 - seg * 8
        first = info[2 + ch] + t0
        q = qd[pl.ds(pos, 2), 0].reshape(2 * BLK, HD)
        do = qd[pl.ds(pos, 2), 1].reshape(2 * BLK, HD)
        qt = q.T
        dot_ = do.T

        def allowed(r):
            if r < BAND:
                return jnp.logical_and(HALO - r + upper < w, first - HALO + r >= 0)
            return info[4 + r - BAND] <= first + upper - w

        def probs(r):
            if r < BAND:
                return pb.at[tt, r * BLK:(r + 1) * BLK]
            return pg.at[tt, (r - BAND) * BLK:(r - BAND + 1) * BLK]

        def grads(r):
            if r < BAND:
                return ds.at[tt, r * BLK:(r + 1) * BLK]
            return dg.at[tt, (r - BAND) * BLK:(r - BAND + 1) * BLK]

        keep = {}

        def scores(r):
            s = dot(kx[ch, t0 + r] if r < BAND else glob[r - BAND, 0], qt)
            if HALO <= r < BAND:
                s = jnp.where(row_full <= lane_full - BLK * (r - HALO), s, NEG)
            st[slot, r * BLK:(r + 1) * BLK] = s
            here = jnp.max(s.reshape(BLK // 8, 8, 2 * BLK), axis=0)
            here = jnp.where(allowed(r), here, NEG)
            keep["top"] = jnp.maximum(keep["top"], here) if r else here

        def after_scores():
            keep["top"] = jnp.max(keep["top"], axis=0, keepdims=True) * c

        def weigh(r):
            off = jnp.where(allowed(r), keep["top"], -NEG)
            e = jnp.exp2(st[slot, r * BLK:(r + 1) * BLK] * c - off)
            here = jnp.sum(e.reshape(BLK // 8, 8, 2 * BLK), axis=0)
            keep["total"] = keep["total"] + here if r else here
            probs(r)[...] = e.astype(BF16)

        cols = pl.ds(pl.multiple_of(t0 * BLK, 2 * BLK), cut)

        def attend():
            keep["inv"] = inv = 1.0 / jnp.sum(keep["total"], axis=0, keepdims=True)
            ot = (dot(vt[ch, :, cols], pb[tt]) + dot(vgt[...], pg[tt])) * inv
            ob = ot.astype(BF16)
            dof = dot_.astype(F32)
            keep["delta"] = jnp.sum(ob.astype(F32) * dof, axis=0, keepdims=True)
            odq[pl.ds(pos, 2), 0] = ob.T.reshape(2, BLK, HD)
            qs[tt] = (qt.astype(F32) * inv).astype(BF16).T
            dos[tt] = (dof * inv).astype(BF16).T

        def back(r):
            v = vx[ch, t0 + r] if r < BAND else glob[r - BAND, 1]
            g = dot(v, dot_) - keep["delta"]
            grads(r)[...] = (probs(r)[...].astype(F32) * g).astype(BF16)

        def finish_tile():
            dqt = (dot(kt[ch, :, cols], ds[tt]) + dot(kgt[...], dg[tt])) * (keep["inv"] * SCALE)
            odq[pl.ds(pos, 2), 1] = dqt.astype(BF16).T.reshape(2, BLK, HD)

        return scores, after_scores, weigh, attend, back, finish_tile

    for ch in range(2):
        def step(i, carry, ch=ch):
            many = range(BAND + GLOB)
            T = [tile(ch, 4 * i + k, k) for k in range(4)]
            S, M, W, A, B, F = [[f[j] for f in T] for j in range(6)]
            for r in many:
                S[0](r)
                S[1](r)
                S[2](r)
                S[3](r)
            M[0]()
            M[1]()
            M[2]()
            M[3]()
            for r in many:
                W[0](r)
                W[1](r)
                W[2](r)
                W[3](r)
            A[0]()
            A[1]()
            A[2]()
            A[3]()
            for r in many:
                B[0](r)
                B[1](r)
                B[2](r)
                B[3](r)
            F[0]()
            F[1]()
            F[2]()
            F[3]()
            return carry

        lax.fori_loop(0, RUN // 2 // 4, step, 0)

        for u in range((EXT + 1) // 2):
            for part, (weights, rows_of) in enumerate(((ds, qs), (pb, dos))):
                acc = [None, None]
                for tt in range(max(0, u - 4), min(RUN // 2, u + 1)):
                    r = 2 * (u - tt)
                    n = min(2, BAND - r)
                    if n == 2:
                        g = dot(weights[tt, r * BLK:(r + 2) * BLK], rows_of[tt])
                        g = [g[:BLK], g[BLK:]]
                    else:
                        g = [dot(weights[tt, r * BLK:(r + 1) * BLK], rows_of[tt])]
                    for k in range(n):
                        acc[k] = g[k] if acc[k] is None else acc[k] + g[k]
                for k in range(2):
                    e = 2 * u + k
                    if e >= EXT or acc[k] is None:
                        continue
                    g = acc[k] * SCALE if part == 0 else acc[k]
                    if ch == 0 and e >= RUN:
                        tail[e - RUN, part] = g
                    if e >= HALO:
                        own[place(ch, e - HALO), part] = g.astype(BF16)
                    elif ch == 0:
                        back_a[e, part] = g.astype(BF16)
                    else:
                        back_b[e, part] = g.astype(BF16)

                        @pl.when(last_y == 1)
                        def _(e=e, part=part, g=g):
                            own[17 + e, part] = (tail[e, part] + g).astype(BF16)
        for part, (weights, rows_of, keep) in enumerate(((dg, qs, dkg), (pg, dos, dvg))):
            acc = None
            for tt in range(RUN // 2):
                g = dot(weights[tt], rows_of[tt])
                acc = g if acc is None else acc + g
            if ch == 0:
                keep[...] = acc
            else:
                acc = acc + keep[...]
                if part == 0:
                    acc = acc * SCALE
                for s in range(GLOB):
                    glob_grad[s, part] = acc[s * BLK:(s + 1) * BLK].astype(BF16)


def place(ch, t):
    return (t // 8) * 16 + t % 8 if ch == 0 else (1 - t // 8) * 16 + 8 + t % 8


def vmem():
    return pl.BlockSpec(memory_space=pltpu.VMEM)


def attention(info, kv, qd, halo_a, halo_b, glob):
    sds = jax.ShapeDtypeStruct
    return pl.pallas_call(
        attention_kernel,
        out_shape=(
            sds((32, 2, BLK, HD), BF16),
            sds((32, 2, BLK, HD), BF16),
            sds((HALO, 2, BLK, HD), BF16),
            sds((HALO, 2, BLK, HD), BF16),
            sds((GLOB, 2, BLK, HD), BF16),
        ),
        in_specs=[pl.BlockSpec(memory_space=pltpu.SMEM)] + [vmem()] * 5,
        out_specs=(vmem(),) * 5,
        scratch_shapes=[
            pltpu.VMEM((2, EXT, BLK, HD), BF16),
            pltpu.VMEM((2, EXT, BLK, HD), BF16),
            pltpu.VMEM((2, HD, EXT * BLK + BLK), BF16),
            pltpu.VMEM((2, HD, EXT * BLK + BLK), BF16),
            pltpu.VMEM((HD, GLOB * BLK), BF16),
            pltpu.VMEM((HD, GLOB * BLK), BF16),
            pltpu.VMEM((RUN // 2, 2 * BLK, HD), BF16),
            pltpu.VMEM((RUN // 2, 2 * BLK, HD), BF16),
            pltpu.VMEM((4, (BAND + GLOB) * BLK, 2 * BLK), F32),
            pltpu.VMEM((RUN // 2, BAND * BLK, 2 * BLK), BF16),
            pltpu.VMEM((RUN // 2, BAND * BLK, 2 * BLK), BF16),
            pltpu.VMEM((RUN // 2, GLOB * BLK, 2 * BLK), BF16),
            pltpu.VMEM((RUN // 2, GLOB * BLK, 2 * BLK), BF16),
            pltpu.VMEM((GLOB * BLK, HD), F32),
            pltpu.VMEM((GLOB * BLK, HD), F32),
            pltpu.VMEM((HALO, 2, BLK, HD), F32),
        ],
        compiler_params=pltpu.CompilerParams(vmem_limit_bytes=52 * 2**20),
        cost_estimate=pl.CostEstimate(
            flops=12 * 448 * BLK**3, bytes_accessed=16 * 2**20, transcendentals=448 * BLK * BLK
        ),
        name="attention",
    )(info, kv, qd, halo_a, halo_b, glob)


def finish_kernel(info, own, back_a, back_b, glob_one, glob_two, out):
    for p in range(32):
        if 17 <= p < 24:
            out[p] = (own[p].astype(F32) + back_a[p - 17].astype(F32)).astype(BF16)
        elif 9 <= p < 16:
            out[p] = (own[p].astype(F32) + back_b[p - 9].astype(F32)).astype(BF16)
        else:
            out[p] = own[p]
    for s in range(GLOB):
        @pl.when(info[16 + s] == 1)
        def _(s=s):
            p = info[10 + s]
            ia = jnp.clip(p - 17, 0, HALO - 1)
            ib = jnp.clip(p - 9, 0, HALO - 1)
            in_a = jnp.logical_and(p >= 17, p < 24)
            in_b = jnp.logical_and(p >= 9, p < 16)
            g = own[p].astype(F32) + glob_one[s].astype(F32) + glob_two[s].astype(F32)
            g = g + jnp.where(in_a, back_a[ia].astype(F32), 0.0)
            g = g + jnp.where(in_b, back_b[ib].astype(F32), 0.0)
            out[p] = g.astype(BF16)


def finish(info, own, back_a, back_b, glob_one, glob_two):
    return pl.pallas_call(
        finish_kernel,
        out_shape=jax.ShapeDtypeStruct((32, 2, BLK, HD), BF16),
        in_specs=[pl.BlockSpec(memory_space=pltpu.SMEM)] + [vmem()] * 5,
        out_specs=vmem(),
        compiler_params=pltpu.CompilerParams(vmem_limit_bytes=16 * 2**20),
        cost_estimate=pl.CostEstimate(flops=2**21, bytes_accessed=6 * 2**20, transcendentals=0),
        name="finish",
    )(info, own, back_a, back_b, glob_one, glob_two)


def to_heads(x, y):
    pair = jnp.stack([x, y], axis=0).reshape(2, BLK, 16, 2, HD)
    pair = jnp.transpose(pair, (3, 2, 0, 1, 4)).reshape(32, 2, BLK, HD)
    return pair


def to_rows(pair):
    pair = pair.reshape(2, 16, 2, BLK, HD)
    pair = jnp.transpose(pair, (2, 3, 1, 0, 4)).reshape(2, BLK, 32, HD)
    return pair[0], pair[1]


def exchange(x):
    return lax.all_to_all(x, GROUP, 0, 0, tiled=True)


PAIR_ONE = [(0, 1), (1, 0), (2, 3), (3, 2)]
PAIR_TWO = [(1, 2), (2, 1), (3, 0), (0, 3)]


def shards(query, keys, values, grad_out, window, global_blocks):
    me = lax.axis_index("y")
    w = jnp.where(lax.axis_index("xh") == 0, window[0], window[1])
    low = global_blocks < 64
    owner = jnp.where(low, global_blocks // RUN, (127 - global_blocks) // RUN)
    t = global_blocks % RUN
    where = jnp.where(low, (t // 8) * 16 + t % 8, (1 - t // 8) * 16 + 8 + t % 8)
    info = jnp.concatenate([
        jnp.stack([w, (me == 3).astype(jnp.int32), RUN * me, 112 - RUN * me]),
        global_blocks, where, (owner == me).astype(jnp.int32),
    ]).astype(jnp.int32)

    kv = exchange(to_heads(keys, values))
    qd = exchange(to_heads(query, grad_out))

    halo_a = lax.ppermute(kv[17:24], "y", [(0, 1), (1, 2), (2, 3)])
    halo_b = lax.ppermute(kv[9:16], "y", [(3, 2), (2, 1), (1, 0)])
    mine = jnp.concatenate([lax.dynamic_slice_in_dim(kv, where[s], 1, 0) for s in range(GLOB)], axis=0)
    other = lax.ppermute(mine, "y", PAIR_ONE)
    mine = jnp.where((owner == me)[:, None, None, None], mine, other)
    other = lax.ppermute(mine, "y", PAIR_TWO)
    glob = jnp.where((owner // 2 == me // 2)[:, None, None, None], mine, other)

    odq, own, back_a, back_b, glob_grad = attention(info, kv, qd, halo_a, halo_b, glob)

    odq = exchange(odq)
    back_a = lax.ppermute(back_a, "y", [(1, 0), (2, 1), (3, 2)])
    back_b = lax.ppermute(back_b, "y", [(0, 1), (1, 2), (2, 3)])
    other = lax.ppermute(glob_grad, "y", PAIR_ONE)
    glob_grad = (glob_grad.astype(F32) + other.astype(F32)).astype(BF16)
    other = lax.ppermute(glob_grad, "y", PAIR_TWO)
    dkv = exchange(finish(info, own, back_a, back_b, glob_grad, other))
    attended, grad_query = to_rows(odq)
    grad_keys, grad_values = to_rows(dkv)
    return attended, grad_query, grad_keys, grad_values


def solution(mesh):
    fine = Mesh(mesh.devices.reshape(4, 2, 2, 4, 2), ("y", "xh", "xl", "z", "c"))
    rows = P(("y", "xh", "xl", "z", "c"), None, None)
    return jax.shard_map(
        shards,
        mesh=fine,
        in_specs=(rows, rows, rows, rows, P(("xl", "z", "c")), P()),
        out_specs=(rows,) * 4,
        check_vma=False,
    )
```

```python
import functools

import jax
import jax.numpy as jnp
from jax import lax
from jax.experimental import pallas as pl
from jax.experimental.pallas import tpu as pltpu
from jax.sharding import Mesh, PartitionSpec as P

BLK = 128
HD = 128
WIN = 8
HALO = WIN - 1
RUN = 16
EXT = HALO + RUN
GLOB = 6
BAND = WIN + 1
UNIT = 3
PART = 3
NEG = -1e30
SCALE = HD ** -0.5
LOG2E = 1.4426950408889634
GROUP = ("xh", "xl", "z", "c")
F32 = jnp.float32
BF16 = jnp.bfloat16


def dot(a, b):
    return jnp.dot(a, b, preferred_element_type=F32)


def attention_kernel(
    info, kv, qd, halo_a, halo_b, glob,
    odq, own, back_a, back_b, glob_grad,
    kx, vx, kt, vt, kgt, vgt, qs, dos, st, pb, ds, pg, dg, dkg, dvg, tail,
):
    w = info[0]
    last_y = info[1]
    for h in range(HALO):
        kx[0, h] = halo_a[h, 0]
        vx[0, h] = halo_a[h, 1]
        kx[1, h] = halo_b[h, 0]
        vx[1, h] = halo_b[h, 1]

    @pl.when(last_y == 1)
    def _():
        for h in range(HALO):
            kx[1, h] = kv[17 + h, 0]
            vx[1, h] = kv[17 + h, 1]

    for t in range(RUN):
        for ch in range(2):
            p = place(ch, t)
            kx[ch, HALO + t] = kv[p, 0]
            vx[ch, HALO + t] = kv[p, 1]
    for e in range(EXT):
        for ch in range(2):
            kt[ch, :, e * BLK:(e + 1) * BLK] = kx[ch, e].T
            vt[ch, :, e * BLK:(e + 1) * BLK] = vx[ch, e].T
    for s in range(GLOB):
        kgt[:, s * BLK:(s + 1) * BLK] = glob[s, 0].T
        vgt[:, s * BLK:(s + 1) * BLK] = glob[s, 1].T

    upper = lax.broadcasted_iota(jnp.int32, (1, 2 * BLK), 1) // BLK
    lane_full = lax.broadcasted_iota(jnp.int32, (BLK, 2 * BLK), 1)
    row_full = lax.broadcasted_iota(jnp.int32, (BLK, 2 * BLK), 0)
    c = SCALE * LOG2E
    cut = BAND * BLK

    def tile(ch, tt, slot, wide):
        t0 = 2 * tt
        seg = tt // 4
        if ch == 0:
            pos = seg * 16 + t0 - seg * 8
        else:
            pos = (1 - seg) * 16 + 8 + t0 - seg * 8
        first = info[2 + ch] + t0
        q = qd[pl.ds(pos, 2), 0].reshape(2 * BLK, HD)
        do = qd[pl.ds(pos, 2), 1].reshape(2 * BLK, HD)
        qt = q.T
        dot_ = do.T

        def allowed(r):
            if r < BAND:
                return jnp.logical_and(HALO - r + upper < w, first - HALO + r >= 0)
            return info[4 + r - BAND] <= first + upper - w

        keep = {}

        def source(ref, which, r, n):
            if r < BAND:
                return ref[ch, pl.ds(t0 + r, n)].reshape(n * BLK, HD)
            return glob[r - BAND:r - BAND + n, which].reshape(n * BLK, HD)

        def probs(r, n):
            if r < BAND:
                return pb.at[tt, r * BLK:(r + n) * BLK]
            return pg.at[slot, (r - BAND) * BLK:(r - BAND + n) * BLK]

        def grads(r, n):
            if r < BAND:
                return ds.at[tt, r * BLK:(r + n) * BLK]
            return dg.at[slot, (r - BAND) * BLK:(r - BAND + n) * BLK]

        def scores(first_r, n):
            big = dot(source(kx, 0, first_r, n), qt)
            for k in range(n):
                r = first_r + k
                s = big[k * BLK:(k + 1) * BLK]
                if HALO <= r < BAND:
                    s = jnp.where(row_full <= lane_full - BLK * (r - HALO), s, NEG)
                st[slot, r * BLK:(r + 1) * BLK] = s
                here = jnp.max(s.reshape(BLK // 8, 8, 2 * BLK), axis=0)
                here = jnp.where(allowed(r), here, NEG)
                keep["top"] = jnp.maximum(keep["top"], here) if r else here

        def after_scores():
            keep["top"] = jnp.max(keep["top"], axis=0, keepdims=True) * c

        def weigh(first_r, n):
            for k in range(n):
                r = first_r + k
                off = jnp.where(allowed(r), keep["top"], -NEG)
                e = jnp.exp2(st[slot, r * BLK:(r + 1) * BLK] * c - off)
                here = jnp.sum(e.reshape(BLK // 8, 8, 2 * BLK), axis=0)
                keep["total"] = keep["total"] + here if r else here
                probs(first_r, n)[k * BLK:(k + 1) * BLK] = e.astype(BF16)

        cols = pl.ds(pl.multiple_of(t0 * BLK, 2 * BLK), cut)

        def attend():
            keep["inv"] = inv = 1.0 / jnp.sum(keep["total"], axis=0, keepdims=True)
            ot = dot(vt[ch, :, cols], pb[tt])
            if wide:
                ot = ot + dot(vgt[:, :wide], pg[slot, :wide])
            ot = ot * inv
            ob = ot.astype(BF16)
            dof = dot_.astype(F32)
            keep["delta"] = jnp.sum(ob.astype(F32) * dof, axis=0, keepdims=True)
            odq[pl.ds(pos, 2), 0] = ob.T.reshape(2, BLK, HD)
            col = jnp.broadcast_to(inv, (8, 2 * BLK)).T[:, :1]
            qs[tt] = (q.astype(F32) * col).astype(BF16)
            dos[tt] = (do.astype(F32) * col).astype(BF16)

        def back(r, n):
            g = dot(source(vx, 1, r, n), dot_) - keep["delta"]
            grads(r, n)[...] = (probs(r, n)[...].astype(F32) * g).astype(BF16)

        def finish_tile():
            dqt = dot(kt[ch, :, cols], ds[tt])
            if wide:
                dqt = dqt + dot(kgt[:, :wide], dg[slot, :wide])
            dqt = dqt * (keep["inv"] * SCALE)
            odq[pl.ds(pos, 2), 1] = dqt.astype(BF16).T.reshape(2, BLK, HD)

        return scores, after_scores, weigh, attend, back, finish_tile

    dkg[...] = jnp.zeros_like(dkg)
    dvg[...] = jnp.zeros_like(dvg)

    def group(ch, i, parts):
        wide = parts * PART * BLK
        segs = [(r, UNIT) for r in range(0, BAND, UNIT)] + [(BAND + PART * k, PART) for k in range(parts)]
        stages = [tile(ch, 4 * i + k, k, wide) for k in range(4)]
        scores, after_scores, weigh, attend, back, finish_tile = zip(*stages)
        for seg in segs:
            for f in scores:
                f(*seg)
        for f in after_scores:
            f()
        for seg in segs:
            for f in weigh:
                f(*seg)
        for f in attend:
            f()
        for seg in segs:
            for f in back:
                f(*seg)
        for f in finish_tile:
            f()
        if parts:
            for weights, rows_of, total in ((dg, qs, dkg), (pg, dos, dvg)):
                acc = total[:wide]
                for k in range(4):
                    acc = acc + dot(weights[k, :wide], rows_of[4 * i + k])
                total[:wide] = acc

    for ch in range(2):
        def step(i, carry, ch=ch):
            last = info[2 + ch] + 8 * i + 7
            count = (info[4] <= last - w).astype(jnp.int32)
            for g in range(1, GLOB):
                count += (info[4 + g] <= last - w).astype(jnp.int32)
            needed = (count + PART - 1) // PART
            for parts in range(GLOB // PART + 1):
                @pl.when(needed == parts)
                def _(parts=parts):
                    group(ch, i, parts)
            return carry

        lax.fori_loop(0, RUN // 8, step, 0)

        for u in range((EXT + 1) // 2):
            for part, (weights, rows_of) in enumerate(((ds, qs), (pb, dos))):
                acc = [None, None]
                for tt in range(max(0, u - 4), min(RUN // 2, u + 1)):
                    r = 2 * (u - tt)
                    n = min(2, BAND - r)
                    if n == 2:
                        g = dot(weights[tt, r * BLK:(r + 2) * BLK], rows_of[tt])
                        g = [g[:BLK], g[BLK:]]
                    else:
                        g = [dot(weights[tt, r * BLK:(r + 1) * BLK], rows_of[tt])]
                    for k in range(n):
                        acc[k] = g[k] if acc[k] is None else acc[k] + g[k]
                for k in range(2):
                    e = 2 * u + k
                    if e >= EXT or acc[k] is None:
                        continue
                    g = acc[k] * SCALE if part == 0 else acc[k]
                    if ch == 0 and e >= RUN:
                        tail[e - RUN, part] = g
                    if e >= HALO:
                        own[place(ch, e - HALO), part] = g.astype(BF16)
                    elif ch == 0:
                        back_a[e, part] = g.astype(BF16)
                    else:
                        back_b[e, part] = g.astype(BF16)

                        @pl.when(last_y == 1)
                        def _(e=e, part=part, g=g):
                            own[17 + e, part] = (tail[e, part] + g).astype(BF16)
    for s in range(GLOB):
        glob_grad[s, 0] = (dkg[s * BLK:(s + 1) * BLK] * SCALE).astype(BF16)
        glob_grad[s, 1] = dvg[s * BLK:(s + 1) * BLK].astype(BF16)


def place(ch, t):
    return (t // 8) * 16 + t % 8 if ch == 0 else (1 - t // 8) * 16 + 8 + t % 8


def vmem():
    return pl.BlockSpec(memory_space=pltpu.VMEM)


def attention(info, kv, qd, halo_a, halo_b, glob):
    sds = jax.ShapeDtypeStruct
    return pl.pallas_call(
        attention_kernel,
        out_shape=(
            sds((32, 2, BLK, HD), BF16),
            sds((32, 2, BLK, HD), BF16),
            sds((HALO, 2, BLK, HD), BF16),
            sds((HALO, 2, BLK, HD), BF16),
            sds((GLOB, 2, BLK, HD), BF16),
        ),
        in_specs=[pl.BlockSpec(memory_space=pltpu.SMEM)] + [vmem()] * 5,
        out_specs=(vmem(),) * 5,
        scratch_shapes=[
            pltpu.VMEM((2, EXT, BLK, HD), BF16),
            pltpu.VMEM((2, EXT, BLK, HD), BF16),
            pltpu.VMEM((2, HD, EXT * BLK + BLK), BF16),
            pltpu.VMEM((2, HD, EXT * BLK + BLK), BF16),
            pltpu.VMEM((HD, GLOB * BLK), BF16),
            pltpu.VMEM((HD, GLOB * BLK), BF16),
            pltpu.VMEM((RUN // 2, 2 * BLK, HD), BF16),
            pltpu.VMEM((RUN // 2, 2 * BLK, HD), BF16),
            pltpu.VMEM((4, (BAND + GLOB) * BLK, 2 * BLK), F32),
            pltpu.VMEM((RUN // 2, BAND * BLK, 2 * BLK), BF16),
            pltpu.VMEM((RUN // 2, BAND * BLK, 2 * BLK), BF16),
            pltpu.VMEM((4, GLOB * BLK, 2 * BLK), BF16),
            pltpu.VMEM((4, GLOB * BLK, 2 * BLK), BF16),
            pltpu.VMEM((GLOB * BLK, HD), F32),
            pltpu.VMEM((GLOB * BLK, HD), F32),
            pltpu.VMEM((HALO, 2, BLK, HD), F32),
        ],
        compiler_params=pltpu.CompilerParams(vmem_limit_bytes=52 * 2**20),
        cost_estimate=pl.CostEstimate(
            flops=12 * 448 * BLK**3, bytes_accessed=16 * 2**20, transcendentals=448 * BLK * BLK
        ),
        name="attention",
    )(info, kv, qd, halo_a, halo_b, glob)


def finish_kernel(info, own, back_a, back_b, glob_one, glob_two, out):
    for p in range(32):
        if 17 <= p < 24:
            out[p] = (own[p].astype(F32) + back_a[p - 17].astype(F32)).astype(BF16)
        elif 9 <= p < 16:
            out[p] = (own[p].astype(F32) + back_b[p - 9].astype(F32)).astype(BF16)
        else:
            out[p] = own[p]
    for s in range(GLOB):
        @pl.when(info[16 + s] == 1)
        def _(s=s):
            p = info[10 + s]
            ia = jnp.clip(p - 17, 0, HALO - 1)
            ib = jnp.clip(p - 9, 0, HALO - 1)
            in_a = jnp.logical_and(p >= 17, p < 24)
            in_b = jnp.logical_and(p >= 9, p < 16)
            g = own[p].astype(F32) + glob_one[s].astype(F32) + glob_two[s].astype(F32)
            g = g + jnp.where(in_a, back_a[ia].astype(F32), 0.0)
            g = g + jnp.where(in_b, back_b[ib].astype(F32), 0.0)
            out[p] = g.astype(BF16)


def finish(info, own, back_a, back_b, glob_one, glob_two):
    return pl.pallas_call(
        finish_kernel,
        out_shape=jax.ShapeDtypeStruct((32, 2, BLK, HD), BF16),
        in_specs=[pl.BlockSpec(memory_space=pltpu.SMEM)] + [vmem()] * 5,
        out_specs=vmem(),
        compiler_params=pltpu.CompilerParams(vmem_limit_bytes=16 * 2**20),
        cost_estimate=pl.CostEstimate(flops=2**21, bytes_accessed=6 * 2**20, transcendentals=0),
        name="finish",
    )(info, own, back_a, back_b, glob_one, glob_two)


def to_heads(x, y):
    pair = jnp.stack([x, y], axis=0).reshape(2, BLK, 16, 2, HD)
    pair = jnp.transpose(pair, (3, 2, 0, 1, 4)).reshape(32, 2, BLK, HD)
    return pair


def to_rows(pair):
    pair = pair.reshape(2, 16, 2, BLK, HD)
    pair = jnp.transpose(pair, (2, 3, 1, 0, 4)).reshape(2, BLK, 32, HD)
    return pair[0], pair[1]


def exchange(x):
    return lax.all_to_all(x, GROUP, 0, 0, tiled=True)


PAIR_ONE = [(0, 1), (1, 0), (2, 3), (3, 2)]
PAIR_TWO = [(1, 2), (2, 1), (3, 0), (0, 3)]


def shards(query, keys, values, grad_out, window, global_blocks):
    me = lax.axis_index("y")
    w = jnp.where(lax.axis_index("xh") == 0, window[0], window[1])
    before = global_blocks[None, :] < global_blocks[:, None]
    rank = jnp.sum(before.astype(jnp.int32), axis=1)
    chosen = rank[None, :] == jnp.arange(GLOB, dtype=jnp.int32)[:, None]
    global_blocks = jnp.sum(jnp.where(chosen, global_blocks[None, :], 0), axis=1)
    low = global_blocks < 64
    owner = jnp.where(low, global_blocks // RUN, (127 - global_blocks) // RUN)
    t = global_blocks % RUN
    where = jnp.where(low, (t // 8) * 16 + t % 8, (1 - t // 8) * 16 + 8 + t % 8)
    info = jnp.concatenate([
        jnp.stack([w, (me == 3).astype(jnp.int32), RUN * me, 112 - RUN * me]),
        global_blocks, where, (owner == me).astype(jnp.int32),
    ]).astype(jnp.int32)

    kv = exchange(to_heads(keys, values))
    qd = exchange(to_heads(query, grad_out))

    halo_a = lax.ppermute(kv[17:24], "y", [(0, 1), (1, 2), (2, 3)])
    halo_b = lax.ppermute(kv[9:16], "y", [(3, 2), (2, 1), (1, 0)])
    mine = jnp.concatenate([lax.dynamic_slice_in_dim(kv, where[s], 1, 0) for s in range(GLOB)], axis=0)
    other = lax.ppermute(mine, "y", PAIR_ONE)
    mine = jnp.where((owner == me)[:, None, None, None], mine, other)
    other = lax.ppermute(mine, "y", PAIR_TWO)
    glob = jnp.where((owner // 2 == me // 2)[:, None, None, None], mine, other)

    odq, own, back_a, back_b, glob_grad = attention(info, kv, qd, halo_a, halo_b, glob)

    odq = exchange(odq)
    back_a = lax.ppermute(back_a, "y", [(1, 0), (2, 1), (3, 2)])
    back_b = lax.ppermute(back_b, "y", [(0, 1), (1, 2), (2, 3)])
    other = lax.ppermute(glob_grad, "y", PAIR_ONE)
    glob_grad = (glob_grad.astype(F32) + other.astype(F32)).astype(BF16)
    other = lax.ppermute(glob_grad, "y", PAIR_TWO)
    dkv = exchange(finish(info, own, back_a, back_b, glob_grad, other))
    attended, grad_query = to_rows(odq)
    grad_keys, grad_values = to_rows(dkv)
    return attended, grad_query, grad_keys, grad_values


def solution(mesh):
    fine = Mesh(mesh.devices.reshape(4, 2, 2, 4, 2), ("y", "xh", "xl", "z", "c"))
    rows = P(("y", "xh", "xl", "z", "c"), None, None)
    return jax.shard_map(
        shards,
        mesh=fine,
        in_specs=(rows, rows, rows, rows, P(("xl", "z", "c")), P()),
        out_specs=(rows,) * 4,
        check_vma=False,
    )
```

```python
import functools

import jax
import jax.numpy as jnp
from jax import lax
from jax.experimental import pallas as pl
from jax.experimental.pallas import tpu as pltpu
from jax.sharding import Mesh, PartitionSpec as P

BLK = 128
HD = 128
WIN = 8
HALO = WIN - 1
RUN = 16
EXT = HALO + RUN
GLOB = 6
BAND = WIN + 1
UNIT = 3
PART = 3
NEG = -1e30
SCALE = HD ** -0.5
LOG2E = 1.4426950408889634
GROUP = ("xh", "xl", "z", "c")
F32 = jnp.float32
BF16 = jnp.bfloat16


def dot(a, b):
    return jnp.dot(a, b, preferred_element_type=F32)


def attention_kernel(
    info, kv, qd, halo_a, halo_b, glob,
    odq, own, back_a, back_b, glob_grad,
    kx, vx, kt, vt, kgt, vgt, qs, dos, st, pb, ds, pg, dg, dkg, dvg, tail, head,
):
    w = info[0]
    last_y = info[1]
    for h in range(HALO):
        kx[0, h] = halo_a[h, 0]
        vx[0, h] = halo_a[h, 1]
        kx[1, h] = halo_b[h, 0]
        vx[1, h] = halo_b[h, 1]

    @pl.when(last_y == 1)
    def _():
        for h in range(HALO):
            kx[1, h] = kv[17 + h, 0]
            vx[1, h] = kv[17 + h, 1]

    for t in range(RUN):
        for ch in range(2):
            p = place(ch, t)
            kx[ch, HALO + t] = kv[p, 0]
            vx[ch, HALO + t] = kv[p, 1]
    for e in range(EXT):
        for ch in range(2):
            kt[ch, :, e * BLK:(e + 1) * BLK] = kx[ch, e].T
            vt[ch, :, e * BLK:(e + 1) * BLK] = vx[ch, e].T
    for s in range(GLOB):
        kgt[:, s * BLK:(s + 1) * BLK] = glob[s, 0].T
        vgt[:, s * BLK:(s + 1) * BLK] = glob[s, 1].T

    upper = lax.broadcasted_iota(jnp.int32, (1, 2 * BLK), 1) // BLK
    lane_full = lax.broadcasted_iota(jnp.int32, (BLK, 2 * BLK), 1)
    row_full = lax.broadcasted_iota(jnp.int32, (BLK, 2 * BLK), 0)
    c = SCALE * LOG2E
    cut = BAND * BLK

    def tile(ch, tt, slot, wide):
        t0 = 2 * tt
        seg = tt // 4
        pos = jnp.where(ch == 0, seg * 16, 24 - seg * 16) + t0 - seg * 8
        first = info[2 + ch] + t0
        q = qd[pl.ds(pos, 2), 0].reshape(2 * BLK, HD)
        do = qd[pl.ds(pos, 2), 1].reshape(2 * BLK, HD)
        qt = q.T
        dot_ = do.T

        def allowed(r):
            if r < BAND:
                return jnp.logical_and(HALO - r + upper < w, first - HALO + r >= 0)
            return info[4 + r - BAND] <= first + upper - w

        keep = {}

        def source(ref, which, r, n):
            if r < BAND:
                return ref[ch, pl.ds(t0 + r, n)].reshape(n * BLK, HD)
            return glob[r - BAND:r - BAND + n, which].reshape(n * BLK, HD)

        def probs(r, n):
            if r < BAND:
                return pb.at[tt, r * BLK:(r + n) * BLK]
            return pg.at[slot, (r - BAND) * BLK:(r - BAND + n) * BLK]

        def grads(r, n):
            if r < BAND:
                return ds.at[tt, r * BLK:(r + n) * BLK]
            return dg.at[slot, (r - BAND) * BLK:(r - BAND + n) * BLK]

        def scores(first_r, n):
            big = dot(source(kx, 0, first_r, n), qt)
            for k in range(n):
                r = first_r + k
                s = big[k * BLK:(k + 1) * BLK]
                if HALO <= r < BAND:
                    s = jnp.where(row_full <= lane_full - BLK * (r - HALO), s, NEG)
                st[slot, r * BLK:(r + 1) * BLK] = s
                here = jnp.max(s.reshape(BLK // 8, 8, 2 * BLK), axis=0)
                here = jnp.where(allowed(r), here, NEG)
                keep["top"] = jnp.maximum(keep["top"], here) if r else here

        def after_scores():
            keep["top"] = jnp.max(keep["top"], axis=0, keepdims=True) * c

        def weigh(first_r, n):
            for k in range(n):
                r = first_r + k
                off = jnp.where(allowed(r), keep["top"], -NEG)
                e = jnp.exp2(st[slot, r * BLK:(r + 1) * BLK] * c - off)
                here = jnp.sum(e.reshape(BLK // 8, 8, 2 * BLK), axis=0)
                keep["total"] = keep["total"] + here if r else here
                probs(first_r, n)[k * BLK:(k + 1) * BLK] = e.astype(BF16)

        cols = pl.ds(pl.multiple_of(t0 * BLK, 2 * BLK), cut)

        def attend():
            keep["inv"] = inv = 1.0 / jnp.sum(keep["total"], axis=0, keepdims=True)
            ot = dot(vt[ch, :, cols], pb[tt])
            if wide:
                ot = ot + dot(vgt[:, :wide], pg[slot, :wide])
            ot = ot * inv
            ob = ot.astype(BF16)
            dof = dot_.astype(F32)
            keep["delta"] = jnp.sum(ob.astype(F32) * dof, axis=0, keepdims=True)
            odq[pl.ds(pos, 2), 0] = ob.T.reshape(2, BLK, HD)
            col = jnp.broadcast_to(inv, (8, 2 * BLK)).T[:, :1]
            qs[tt] = (q.astype(F32) * col).astype(BF16)
            dos[tt] = (do.astype(F32) * col).astype(BF16)

        def back(r, n):
            g = dot(source(vx, 1, r, n), dot_) - keep["delta"]
            grads(r, n)[...] = (probs(r, n)[...].astype(F32) * g).astype(BF16)

        def finish_tile():
            dqt = dot(kt[ch, :, cols], ds[tt])
            if wide:
                dqt = dqt + dot(kgt[:, :wide], dg[slot, :wide])
            dqt = dqt * (keep["inv"] * SCALE)
            odq[pl.ds(pos, 2), 1] = dqt.astype(BF16).T.reshape(2, BLK, HD)

        return scores, after_scores, weigh, attend, back, finish_tile

    dkg[...] = jnp.zeros_like(dkg)
    dvg[...] = jnp.zeros_like(dvg)

    def group(ch, i, parts):
        wide = parts * PART * BLK
        segs = [(r, UNIT) for r in range(0, BAND, UNIT)] + [(BAND + PART * k, PART) for k in range(parts)]
        stages = [tile(ch, 4 * i + k, k, wide) for k in range(4)]
        scores, after_scores, weigh, attend, back, finish_tile = zip(*stages)
        for seg in segs:
            for f in scores:
                f(*seg)
        for f in after_scores:
            f()
        for seg in segs:
            for f in weigh:
                f(*seg)
        for f in attend:
            f()
        for seg in segs:
            for f in back:
                f(*seg)
        for f in finish_tile:
            f()
        if parts:
            for weights, rows_of, total in ((dg, qs, dkg), (pg, dos, dvg)):
                acc = total[:wide]
                for k in range(4):
                    acc = acc + dot(weights[k, :wide], rows_of[4 * i + k])
                total[:wide] = acc

    def run(ch, outer):
        def step(i, carry):
            last = info[2 + ch] + 8 * i + 7
            count = (info[4] <= last - w).astype(jnp.int32)
            for g in range(1, GLOB):
                count += (info[4 + g] <= last - w).astype(jnp.int32)
            needed = (count + PART - 1) // PART
            for parts in range(GLOB // PART + 1):
                @pl.when(needed == parts)
                def _(parts=parts):
                    group(ch, i, parts)
            return carry

        lax.fori_loop(0, RUN // 8, step, 0)

        for u in range((EXT + 1) // 2):
            for part, (weights, rows_of) in enumerate(((ds, qs), (pb, dos))):
                acc = [None, None]
                for tt in range(max(0, u - 4), min(RUN // 2, u + 1)):
                    r = 2 * (u - tt)
                    n = min(2, BAND - r)
                    if n == 2:
                        g = dot(weights[tt, r * BLK:(r + 2) * BLK], rows_of[tt])
                        g = [g[:BLK], g[BLK:]]
                    else:
                        g = [dot(weights[tt, r * BLK:(r + 1) * BLK], rows_of[tt])]
                    for k in range(n):
                        acc[k] = g[k] if acc[k] is None else acc[k] + g[k]
                for k in range(2):
                    e = 2 * u + k
                    if e >= EXT or acc[k] is None:
                        continue
                    g = acc[k] * SCALE if part == 0 else acc[k]
                    if e < HALO:
                        head[ch, e, part] = g
                    else:
                        t = e - HALO
                        own[jnp.where(ch == 0, place(0, t), place(1, t)), part] = g.astype(BF16)
                    if e >= RUN:
                        tail[ch, e - RUN, part] = g
        return outer

    lax.fori_loop(0, 2, run, 0)
    for h in range(HALO):
        back_a[h] = head[0, h].astype(BF16)
        back_b[h] = head[1, h].astype(BF16)

    @pl.when(last_y == 1)
    def _():
        for h in range(HALO):
            own[17 + h] = (tail[0, h] + head[1, h]).astype(BF16)

    for s in range(GLOB):
        glob_grad[s, 0] = (dkg[s * BLK:(s + 1) * BLK] * SCALE).astype(BF16)
        glob_grad[s, 1] = dvg[s * BLK:(s + 1) * BLK].astype(BF16)


def place(ch, t):
    return (t // 8) * 16 + t % 8 if ch == 0 else (1 - t // 8) * 16 + 8 + t % 8


def vmem():
    return pl.BlockSpec(memory_space=pltpu.VMEM)


def attention(info, kv, qd, halo_a, halo_b, glob):
    sds = jax.ShapeDtypeStruct
    return pl.pallas_call(
        attention_kernel,
        out_shape=(
            sds((32, 2, BLK, HD), BF16),
            sds((32, 2, BLK, HD), BF16),
            sds((HALO, 2, BLK, HD), BF16),
            sds((HALO, 2, BLK, HD), BF16),
            sds((GLOB, 2, BLK, HD), BF16),
        ),
        in_specs=[pl.BlockSpec(memory_space=pltpu.SMEM)] + [vmem()] * 5,
        out_specs=(vmem(),) * 5,
        scratch_shapes=[
            pltpu.VMEM((2, EXT, BLK, HD), BF16),
            pltpu.VMEM((2, EXT, BLK, HD), BF16),
            pltpu.VMEM((2, HD, EXT * BLK + BLK), BF16),
            pltpu.VMEM((2, HD, EXT * BLK + BLK), BF16),
            pltpu.VMEM((HD, GLOB * BLK), BF16),
            pltpu.VMEM((HD, GLOB * BLK), BF16),
            pltpu.VMEM((RUN // 2, 2 * BLK, HD), BF16),
            pltpu.VMEM((RUN // 2, 2 * BLK, HD), BF16),
            pltpu.VMEM((4, (BAND + GLOB) * BLK, 2 * BLK), F32),
            pltpu.VMEM((RUN // 2, BAND * BLK, 2 * BLK), BF16),
            pltpu.VMEM((RUN // 2, BAND * BLK, 2 * BLK), BF16),
            pltpu.VMEM((4, GLOB * BLK, 2 * BLK), BF16),
            pltpu.VMEM((4, GLOB * BLK, 2 * BLK), BF16),
            pltpu.VMEM((GLOB * BLK, HD), F32),
            pltpu.VMEM((GLOB * BLK, HD), F32),
            pltpu.VMEM((2, HALO, 2, BLK, HD), F32),
            pltpu.VMEM((2, HALO, 2, BLK, HD), F32),
        ],
        compiler_params=pltpu.CompilerParams(vmem_limit_bytes=52 * 2**20),
        cost_estimate=pl.CostEstimate(
            flops=12 * 448 * BLK**3, bytes_accessed=16 * 2**20, transcendentals=448 * BLK * BLK
        ),
        name="attention",
    )(info, kv, qd, halo_a, halo_b, glob)


def finish_kernel(info, own, back_a, back_b, glob_one, glob_two, out):
    for p in range(32):
        if 17 <= p < 24:
            out[p] = (own[p].astype(F32) + back_a[p - 17].astype(F32)).astype(BF16)
        elif 9 <= p < 16:
            out[p] = (own[p].astype(F32) + back_b[p - 9].astype(F32)).astype(BF16)
        else:
            out[p] = own[p]
    for s in range(GLOB):
        @pl.when(info[16 + s] == 1)
        def _(s=s):
            p = info[10 + s]
            ia = jnp.clip(p - 17, 0, HALO - 1)
            ib = jnp.clip(p - 9, 0, HALO - 1)
            in_a = jnp.logical_and(p >= 17, p < 24)
            in_b = jnp.logical_and(p >= 9, p < 16)
            g = own[p].astype(F32) + glob_one[s].astype(F32) + glob_two[s].astype(F32)
            g = g + jnp.where(in_a, back_a[ia].astype(F32), 0.0)
            g = g + jnp.where(in_b, back_b[ib].astype(F32), 0.0)
            out[p] = g.astype(BF16)


def finish(info, own, back_a, back_b, glob_one, glob_two):
    return pl.pallas_call(
        finish_kernel,
        out_shape=jax.ShapeDtypeStruct((32, 2, BLK, HD), BF16),
        in_specs=[pl.BlockSpec(memory_space=pltpu.SMEM)] + [vmem()] * 5,
        out_specs=vmem(),
        compiler_params=pltpu.CompilerParams(vmem_limit_bytes=16 * 2**20),
        cost_estimate=pl.CostEstimate(flops=2**21, bytes_accessed=6 * 2**20, transcendentals=0),
        name="finish",
    )(info, own, back_a, back_b, glob_one, glob_two)


def to_heads(x, y):
    pair = jnp.stack([x, y], axis=0).reshape(2, BLK, 16, 2, HD)
    pair = jnp.transpose(pair, (3, 2, 0, 1, 4)).reshape(32, 2, BLK, HD)
    return pair


def to_rows(pair):
    pair = pair.reshape(2, 16, 2, BLK, HD)
    pair = jnp.transpose(pair, (2, 3, 1, 0, 4)).reshape(2, BLK, 32, HD)
    return pair[0], pair[1]


def exchange(x):
    return lax.all_to_all(x, GROUP, 0, 0, tiled=True)


PAIR_ONE = [(0, 1), (1, 0), (2, 3), (3, 2)]
PAIR_TWO = [(1, 2), (2, 1), (3, 0), (0, 3)]


def shards(query, keys, values, grad_out, window, global_blocks):
    me = lax.axis_index("y")
    w = jnp.where(lax.axis_index("xh") == 0, window[0], window[1])
    before = global_blocks[None, :] < global_blocks[:, None]
    rank = jnp.sum(before.astype(jnp.int32), axis=1)
    chosen = rank[None, :] == jnp.arange(GLOB, dtype=jnp.int32)[:, None]
    global_blocks = jnp.sum(jnp.where(chosen, global_blocks[None, :], 0), axis=1)
    low = global_blocks < 64
    owner = jnp.where(low, global_blocks // RUN, (127 - global_blocks) // RUN)
    t = global_blocks % RUN
    where = jnp.where(low, (t // 8) * 16 + t % 8, (1 - t // 8) * 16 + 8 + t % 8)
    info = jnp.concatenate([
        jnp.stack([w, (me == 3).astype(jnp.int32), RUN * me, 112 - RUN * me]),
        global_blocks, where, (owner == me).astype(jnp.int32),
    ]).astype(jnp.int32)

    kv = exchange(to_heads(keys, values))
    qd = exchange(to_heads(query, grad_out))

    halo_a = lax.ppermute(kv[17:24], "y", [(0, 1), (1, 2), (2, 3)])
    halo_b = lax.ppermute(kv[9:16], "y", [(3, 2), (2, 1), (1, 0)])
    mine = jnp.concatenate([lax.dynamic_slice_in_dim(kv, where[s], 1, 0) for s in range(GLOB)], axis=0)
    other = lax.ppermute(mine, "y", PAIR_ONE)
    mine = jnp.where((owner == me)[:, None, None, None], mine, other)
    other = lax.ppermute(mine, "y", PAIR_TWO)
    glob = jnp.where((owner // 2 == me // 2)[:, None, None, None], mine, other)

    odq, own, back_a, back_b, glob_grad = attention(info, kv, qd, halo_a, halo_b, glob)

    odq = exchange(odq)
    back_a = lax.ppermute(back_a, "y", [(1, 0), (2, 1), (3, 2)])
    back_b = lax.ppermute(back_b, "y", [(0, 1), (1, 2), (2, 3)])
    other = lax.ppermute(glob_grad, "y", PAIR_ONE)
    glob_grad = (glob_grad.astype(F32) + other.astype(F32)).astype(BF16)
    other = lax.ppermute(glob_grad, "y", PAIR_TWO)
    dkv = exchange(finish(info, own, back_a, back_b, glob_grad, other))
    attended, grad_query = to_rows(odq)
    grad_keys, grad_values = to_rows(dkv)
    return attended, grad_query, grad_keys, grad_values


def solution(mesh):
    fine = Mesh(mesh.devices.reshape(4, 2, 2, 4, 2), ("y", "xh", "xl", "z", "c"))
    rows = P(("y", "xh", "xl", "z", "c"), None, None)
    return jax.shard_map(
        shards,
        mesh=fine,
        in_specs=(rows, rows, rows, rows, P(("xl", "z", "c")), P()),
        out_specs=(rows,) * 4,
        check_vma=False,
    )
```

```python
import functools

import jax
import jax.numpy as jnp
from jax import lax
from jax.experimental import pallas as pl
from jax.experimental.pallas import tpu as pltpu
from jax.sharding import Mesh, PartitionSpec as P

BLK = 128
HD = 128
WIN = 8
HALO = WIN - 1
RUN = 16
EXT = HALO + RUN
GLOB = 6
BAND = WIN + 1
UNIT = 3
PART = 3
NEG = -1e30
SCALE = HD ** -0.5
LOG2E = 1.4426950408889634
GROUP = ("xh", "xl", "z", "c")
F32 = jnp.float32
BF16 = jnp.bfloat16


def dot(a, b):
    return jnp.dot(a, b, preferred_element_type=F32)


def attention_kernel(
    info, kv, qd, halo_a, halo_b, glob,
    odq, own, back_a, back_b, glob_grad,
    kx, vx, kt, vt, kgt, vgt, qs, dos, st, pb, ds, pg, dg, dkg, dvg, tail, head,
):
    w = info[0]
    last_y = info[1]
    for h in range(HALO):
        kx[0, h] = halo_a[h, 0]
        vx[0, h] = halo_a[h, 1]
        kx[1, h] = halo_b[h, 0]
        vx[1, h] = halo_b[h, 1]

    @pl.when(last_y == 1)
    def _():
        for h in range(HALO):
            kx[1, h] = kv[17 + h, 0]
            vx[1, h] = kv[17 + h, 1]

    for t in range(RUN):
        for ch in range(2):
            p = place(ch, t)
            kx[ch, HALO + t] = kv[p, 0]
            vx[ch, HALO + t] = kv[p, 1]
    for e in range(EXT):
        for ch in range(2):
            kt[ch, :, e * BLK:(e + 1) * BLK] = kx[ch, e].T
            vt[ch, :, e * BLK:(e + 1) * BLK] = vx[ch, e].T
    for s in range(GLOB):
        kgt[:, s * BLK:(s + 1) * BLK] = glob[s, 0].T
        vgt[:, s * BLK:(s + 1) * BLK] = glob[s, 1].T

    upper = lax.broadcasted_iota(jnp.int32, (1, 2 * BLK), 1) // BLK
    lane_full = lax.broadcasted_iota(jnp.int32, (BLK, 2 * BLK), 1)
    row_full = lax.broadcasted_iota(jnp.int32, (BLK, 2 * BLK), 0)
    c = SCALE * LOG2E
    cut = BAND * BLK

    def tile(ch, tt, slot, wide):
        t0 = 2 * tt
        seg = tt // 4
        pos = jnp.where(ch == 0, seg * 16, 24 - seg * 16) + t0 - seg * 8
        first = info[2 + ch] + t0
        q = qd[pl.ds(pos, 2), 0].reshape(2 * BLK, HD)
        do = qd[pl.ds(pos, 2), 1].reshape(2 * BLK, HD)
        qt = q.T
        dot_ = do.T

        def allowed(r):
            if r < BAND:
                return jnp.logical_and(HALO - r + upper < w, first - HALO + r >= 0)
            return info[4 + r - BAND] <= first + upper - w

        keep = {}

        def source(ref, which, r, n):
            if r < BAND:
                return ref[ch, pl.ds(t0 + r, n)].reshape(n * BLK, HD)
            return glob[r - BAND:r - BAND + n, which].reshape(n * BLK, HD)

        def probs(r, n):
            if r < BAND:
                return pb.at[tt, r * BLK:(r + n) * BLK]
            return pg.at[slot, (r - BAND) * BLK:(r - BAND + n) * BLK]

        def grads(r, n):
            if r < BAND:
                return ds.at[tt, r * BLK:(r + n) * BLK]
            return dg.at[slot, (r - BAND) * BLK:(r - BAND + n) * BLK]

        def scores(first_r, n):
            big = dot(source(kx, 0, first_r, n), qt)
            for k in range(n):
                r = first_r + k
                s = big[k * BLK:(k + 1) * BLK]
                if HALO <= r < BAND:
                    s = jnp.where(row_full <= lane_full - BLK * (r - HALO), s, NEG)
                st[slot, r * BLK:(r + 1) * BLK] = s
                here = jnp.max(s.reshape(BLK // 8, 8, 2 * BLK), axis=0)
                here = jnp.where(allowed(r), here, NEG)
                keep["top"] = jnp.maximum(keep["top"], here) if r else here

        def after_scores():
            keep["top"] = jnp.max(keep["top"], axis=0, keepdims=True) * c

        def weigh(first_r, n):
            for k in range(n):
                r = first_r + k
                off = jnp.where(allowed(r), keep["top"], -NEG)
                e = jnp.exp2(st[slot, r * BLK:(r + 1) * BLK] * c - off)
                here = jnp.sum(e.reshape(BLK // 8, 8, 2 * BLK), axis=0)
                keep["total"] = keep["total"] + here if r else here
                probs(first_r, n)[k * BLK:(k + 1) * BLK] = e.astype(BF16)

        cols = pl.ds(pl.multiple_of(t0 * BLK, 2 * BLK), cut)

        def attend():
            keep["inv"] = inv = 1.0 / jnp.sum(keep["total"], axis=0, keepdims=True)
            ot = dot(vt[ch, :, cols], pb[tt])
            if wide:
                ot = ot + dot(vgt[:, :wide], pg[slot, :wide])
            ot = ot * inv
            ob = ot.astype(BF16)
            dof = dot_.astype(F32)
            keep["delta"] = jnp.sum(ob.astype(F32) * dof, axis=0, keepdims=True)
            odq[pl.ds(pos, 2), 0] = ob.T.reshape(2, BLK, HD)
            col = jnp.broadcast_to(inv, (8, 2 * BLK)).T[:, :1]
            qs[tt] = (q.astype(F32) * col).astype(BF16)
            dos[tt] = (do.astype(F32) * col).astype(BF16)

        def back(r, n):
            g = dot(source(vx, 1, r, n), dot_) - keep["delta"]
            grads(r, n)[...] = (probs(r, n)[...].astype(F32) * g).astype(BF16)

        def finish_tile():
            dqt = dot(kt[ch, :, cols], ds[tt])
            if wide:
                dqt = dqt + dot(kgt[:, :wide], dg[slot, :wide])
            dqt = dqt * (keep["inv"] * SCALE)
            odq[pl.ds(pos, 2), 1] = dqt.astype(BF16).T.reshape(2, BLK, HD)

        return scores, after_scores, weigh, attend, back, finish_tile

    dkg[...] = jnp.zeros_like(dkg)
    dvg[...] = jnp.zeros_like(dvg)

    def group(ch, i, parts):
        wide = parts * PART * BLK
        segs = [(r, UNIT) for r in range(0, BAND, UNIT)] + [(BAND + PART * k, PART) for k in range(parts)]
        stages = [tile(ch, 4 * i + k, k, wide) for k in range(4)]
        scores, after_scores, weigh, attend, back, finish_tile = zip(*stages)
        for seg in segs:
            for f in scores:
                f(*seg)
        for f in after_scores:
            f()
        for seg in segs:
            for f in weigh:
                f(*seg)
        for f in attend:
            f()
        for seg in segs:
            for f in back:
                f(*seg)
        for f in finish_tile:
            f()
        if parts:
            for weights, rows_of, total in ((dg, qs, dkg), (pg, dos, dvg)):
                acc = total[:wide]
                for k in range(4):
                    acc = acc + dot(weights[k, :wide], rows_of[4 * i + k])
                total[:wide] = acc

    def run(ch, outer):
        def step(i, carry):
            last = info[2 + ch] + 8 * i + 7
            count = (info[4] <= last - w).astype(jnp.int32)
            for g in range(1, GLOB):
                count += (info[4 + g] <= last - w).astype(jnp.int32)
            needed = (count + PART - 1) // PART
            for parts in range(GLOB // PART + 1):
                @pl.when(needed == parts)
                def _(parts=parts):
                    group(ch, i, parts)
            return carry

        lax.fori_loop(0, RUN // 8, step, 0)

        for u in range((EXT + 1) // 2):
            for part, (weights, rows_of) in enumerate(((ds, qs), (pb, dos))):
                acc = [None, None]
                for tt in range(max(0, u - 4), min(RUN // 2, u + 1)):
                    r = 2 * (u - tt)
                    n = min(2, BAND - r)
                    if n == 2:
                        g = dot(weights[tt, r * BLK:(r + 2) * BLK], rows_of[tt])
                        g = [g[:BLK], g[BLK:]]
                    else:
                        g = [dot(weights[tt, r * BLK:(r + 1) * BLK], rows_of[tt])]
                    for k in range(n):
                        acc[k] = g[k] if acc[k] is None else acc[k] + g[k]
                for k in range(2):
                    e = 2 * u + k
                    if e >= EXT or acc[k] is None:
                        continue
                    g = acc[k] * SCALE if part == 0 else acc[k]
                    if e < HALO:
                        head[ch, e, part] = g
                    else:
                        t = e - HALO
                        own[jnp.where(ch == 0, place(0, t), place(1, t)), part] = g.astype(BF16)
                    if e >= RUN:
                        tail[ch, e - RUN, part] = g
        return outer

    lax.fori_loop(0, 2, run, 0)
    for h in range(HALO):
        back_a[h] = head[0, h].astype(BF16)
        back_b[h] = head[1, h].astype(BF16)

    @pl.when(last_y == 1)
    def _():
        for h in range(HALO):
            own[17 + h] = (tail[0, h] + head[1, h]).astype(BF16)

    for s in range(GLOB):
        glob_grad[s, 0] = (dkg[s * BLK:(s + 1) * BLK] * SCALE).astype(BF16)
        glob_grad[s, 1] = dvg[s * BLK:(s + 1) * BLK].astype(BF16)


def place(ch, t):
    return (t // 8) * 16 + t % 8 if ch == 0 else (1 - t // 8) * 16 + 8 + t % 8


def vmem():
    return pl.BlockSpec(memory_space=pltpu.VMEM)


def attention(info, kv, qd, halo_a, halo_b, glob):
    sds = jax.ShapeDtypeStruct
    return pl.pallas_call(
        attention_kernel,
        out_shape=(
            sds((32, 2, BLK, HD), BF16),
            sds((32, 2, BLK, HD), BF16),
            sds((HALO, 2, BLK, HD), BF16),
            sds((HALO, 2, BLK, HD), BF16),
            sds((GLOB, 2, BLK, HD), BF16),
        ),
        in_specs=[pl.BlockSpec(memory_space=pltpu.SMEM)] + [vmem()] * 5,
        out_specs=(vmem(),) * 5,
        scratch_shapes=[
            pltpu.VMEM((2, EXT, BLK, HD), BF16),
            pltpu.VMEM((2, EXT, BLK, HD), BF16),
            pltpu.VMEM((2, HD, EXT * BLK + BLK), BF16),
            pltpu.VMEM((2, HD, EXT * BLK + BLK), BF16),
            pltpu.VMEM((HD, GLOB * BLK), BF16),
            pltpu.VMEM((HD, GLOB * BLK), BF16),
            pltpu.VMEM((RUN // 2, 2 * BLK, HD), BF16),
            pltpu.VMEM((RUN // 2, 2 * BLK, HD), BF16),
            pltpu.VMEM((4, (BAND + GLOB) * BLK, 2 * BLK), F32),
            pltpu.VMEM((RUN // 2, BAND * BLK, 2 * BLK), BF16),
            pltpu.VMEM((RUN // 2, BAND * BLK, 2 * BLK), BF16),
            pltpu.VMEM((4, GLOB * BLK, 2 * BLK), BF16),
            pltpu.VMEM((4, GLOB * BLK, 2 * BLK), BF16),
            pltpu.VMEM((GLOB * BLK, HD), F32),
            pltpu.VMEM((GLOB * BLK, HD), F32),
            pltpu.VMEM((2, HALO, 2, BLK, HD), F32),
            pltpu.VMEM((2, HALO, 2, BLK, HD), F32),
        ],
        compiler_params=pltpu.CompilerParams(vmem_limit_bytes=52 * 2**20),
        cost_estimate=pl.CostEstimate(
            flops=12 * 448 * BLK**3, bytes_accessed=16 * 2**20, transcendentals=448 * BLK * BLK
        ),
        name="attention",
    )(info, kv, qd, halo_a, halo_b, glob)


def finish_kernel(info, own, back_a, back_b, glob_one, glob_two, out):
    for p in range(32):
        if 17 <= p < 24:
            out[p] = (own[p].astype(F32) + back_a[p - 17].astype(F32)).astype(BF16)
        elif 9 <= p < 16:
            out[p] = (own[p].astype(F32) + back_b[p - 9].astype(F32)).astype(BF16)
        else:
            out[p] = own[p]
    for s in range(GLOB):
        @pl.when(info[16 + s] == 1)
        def _(s=s):
            p = info[10 + s]
            ia = jnp.clip(p - 17, 0, HALO - 1)
            ib = jnp.clip(p - 9, 0, HALO - 1)
            in_a = jnp.logical_and(p >= 17, p < 24)
            in_b = jnp.logical_and(p >= 9, p < 16)
            g = own[p].astype(F32) + glob_one[s].astype(F32) + glob_two[s].astype(F32)
            g = g + jnp.where(in_a, back_a[ia].astype(F32), 0.0)
            g = g + jnp.where(in_b, back_b[ib].astype(F32), 0.0)
            out[p] = g.astype(BF16)


def finish(info, own, back_a, back_b, glob_one, glob_two):
    return pl.pallas_call(
        finish_kernel,
        out_shape=jax.ShapeDtypeStruct((32, 2, BLK, HD), BF16),
        in_specs=[pl.BlockSpec(memory_space=pltpu.SMEM)] + [vmem()] * 5,
        out_specs=vmem(),
        compiler_params=pltpu.CompilerParams(vmem_limit_bytes=16 * 2**20),
        cost_estimate=pl.CostEstimate(flops=2**21, bytes_accessed=6 * 2**20, transcendentals=0),
        name="finish",
    )(info, own, back_a, back_b, glob_one, glob_two)


def to_heads(x, y):
    pair = jnp.stack([x, y], axis=0).reshape(2, BLK, 16, 2, HD)
    pair = jnp.transpose(pair, (3, 2, 0, 1, 4)).reshape(32, 2, BLK, HD)
    return pair


def to_rows(pair):
    pair = pair.reshape(2, 16, 2, BLK, HD)
    pair = jnp.transpose(pair, (2, 3, 1, 0, 4)).reshape(2, BLK, 32, HD)
    return pair[0], pair[1]


def exchange(x):
    return lax.all_to_all(x, GROUP, 0, 0, tiled=True)


PAIR_ONE = [(0, 1), (1, 0), (2, 3), (3, 2)]
PAIR_TWO = [(1, 2), (2, 1), (3, 0), (0, 3)]


def shards(query, keys, values, grad_out, window, global_blocks):
    me = lax.axis_index("y")
    w = jnp.where(lax.axis_index("xh") == 0, window[0], window[1])
    before = global_blocks[None, :] < global_blocks[:, None]
    rank = jnp.sum(before.astype(jnp.int32), axis=1)
    chosen = rank[None, :] == jnp.arange(GLOB, dtype=jnp.int32)[:, None]
    global_blocks = jnp.sum(jnp.where(chosen, global_blocks[None, :], 0), axis=1)
    low = global_blocks < 64
    owner = jnp.where(low, global_blocks // RUN, (127 - global_blocks) // RUN)
    t = global_blocks % RUN
    where = jnp.where(low, (t // 8) * 16 + t % 8, (1 - t // 8) * 16 + 8 + t % 8)
    info = jnp.concatenate([
        jnp.stack([w, (me == 3).astype(jnp.int32), RUN * me, 112 - RUN * me]),
        global_blocks, where, (owner == me).astype(jnp.int32),
    ]).astype(jnp.int32)

    kv = exchange(to_heads(keys, values))
    qd = exchange(to_heads(query, grad_out))

    halo_a = lax.ppermute(kv[17:24], "y", [(0, 1), (1, 2), (2, 3)])
    halo_b = lax.ppermute(kv[9:16], "y", [(3, 2), (2, 1), (1, 0)])
    mine = jnp.concatenate([lax.dynamic_slice_in_dim(kv, where[s], 1, 0) for s in range(GLOB)], axis=0)
    other = lax.ppermute(mine, "y", PAIR_ONE)
    halo_a, halo_b, other = lax.optimization_barrier((halo_a, halo_b, other))
    mine = jnp.where((owner == me)[:, None, None, None], mine, other)
    other = lax.ppermute(mine, "y", PAIR_TWO)
    glob = jnp.where((owner // 2 == me // 2)[:, None, None, None], mine, other)

    odq, own, back_a, back_b, glob_grad = attention(info, kv, qd, halo_a, halo_b, glob)

    odq = exchange(odq)
    back_a = lax.ppermute(back_a, "y", [(1, 0), (2, 1), (3, 2)])
    back_b = lax.ppermute(back_b, "y", [(0, 1), (1, 2), (2, 3)])
    other = lax.ppermute(glob_grad, "y", PAIR_ONE)
    glob_grad = (glob_grad.astype(F32) + other.astype(F32)).astype(BF16)
    other = lax.ppermute(glob_grad, "y", PAIR_TWO)
    dkv = exchange(finish(info, own, back_a, back_b, glob_grad, other))
    attended, grad_query = to_rows(odq)
    grad_keys, grad_values = to_rows(dkv)
    return attended, grad_query, grad_keys, grad_values


def solution(mesh):
    fine = Mesh(mesh.devices.reshape(4, 2, 2, 4, 2), ("y", "xh", "xl", "z", "c"))
    rows = P(("y", "xh", "xl", "z", "c"), None, None)
    return jax.shard_map(
        shards,
        mesh=fine,
        in_specs=(rows, rows, rows, rows, P(("xl", "z", "c")), P()),
        out_specs=(rows,) * 4,
        check_vma=False,
    )
```

```python
import functools

import jax
import jax.numpy as jnp
from jax import lax
from jax.experimental import pallas as pl
from jax.experimental.pallas import tpu as pltpu
from jax.sharding import Mesh, PartitionSpec as P

BLK = 128
HD = 128
WIN = 8
HALO = WIN - 1
RUN = 16
EXT = HALO + RUN
GLOB = 6
BAND = WIN + 1
UNIT = 3
STEPS = (3, 5, 6)
ONES = 16
NEG = -1e30
SCALE = HD ** -0.5
LOG2E = 1.4426950408889634
GROUP = ("xh", "xl", "z", "c")
F32 = jnp.float32
BF16 = jnp.bfloat16


def dot(a, b):
    return jnp.dot(a, b, preferred_element_type=F32)


def attention_kernel(
    info, kv, qd, halo_a, halo_b, glob,
    odq, own, back_a, back_b, glob_grad,
    kx, vx, kt, vt, kgt, vgt, qs, dos, st, pb, ds, pg, dg, dkg, dvg, tail, head,
):
    w = info[0]
    last_y = info[1]
    for h in range(HALO):
        kx[0, h] = halo_a[h, 0]
        vx[0, h] = halo_a[h, 1]
        kx[1, h] = halo_b[h, 0]
        vx[1, h] = halo_b[h, 1]

    @pl.when(last_y == 1)
    def _():
        for h in range(HALO):
            kx[1, h] = kv[17 + h, 0]
            vx[1, h] = kv[17 + h, 1]

    for t in range(RUN):
        for ch in range(2):
            p = place(ch, t)
            kx[ch, HALO + t] = kv[p, 0]
            vx[ch, HALO + t] = kv[p, 1]
    for e in range(EXT):
        for ch in range(2):
            kt[ch, :, e * BLK:(e + 1) * BLK] = kx[ch, e].T
            vt[ch, :HD, e * BLK:(e + 1) * BLK] = vx[ch, e].T
    for s in range(GLOB):
        kgt[:, s * BLK:(s + 1) * BLK] = glob[s, 0].T
        vgt[:HD, s * BLK:(s + 1) * BLK] = glob[s, 1].T

    upper = lax.broadcasted_iota(jnp.int32, (1, 2 * BLK), 1) // BLK
    lane_full = lax.broadcasted_iota(jnp.int32, (BLK, 2 * BLK), 1)
    row_full = lax.broadcasted_iota(jnp.int32, (BLK, 2 * BLK), 0)
    c = SCALE * LOG2E
    cut = BAND * BLK

    def tile(ch, tt, slot, wide):
        t0 = 2 * tt
        seg = tt // 4
        pos = jnp.where(ch == 0, seg * 16, 24 - seg * 16) + t0 - seg * 8
        first = info[2 + ch] + t0
        q = qd[pl.ds(pos, 2), 0].reshape(2 * BLK, HD)
        do = qd[pl.ds(pos, 2), 1].reshape(2 * BLK, HD)
        qt = q.T
        dot_ = do.T

        def allowed(r):
            if r < BAND:
                return jnp.logical_and(HALO - r + upper < w, first - HALO + r >= 0)
            return info[4 + r - BAND] <= first + upper - w

        keep = {}

        def source(ref, which, r, n):
            if r < BAND:
                return ref[ch, pl.ds(t0 + r, n)].reshape(n * BLK, HD)
            return glob[r - BAND:r - BAND + n, which].reshape(n * BLK, HD)

        def probs(r, n):
            if r < BAND:
                return pb.at[tt, r * BLK:(r + n) * BLK]
            return pg.at[slot, (r - BAND) * BLK:(r - BAND + n) * BLK]

        def grads(r, n):
            if r < BAND:
                return ds.at[tt, r * BLK:(r + n) * BLK]
            return dg.at[slot, (r - BAND) * BLK:(r - BAND + n) * BLK]

        def scores(first_r, n):
            big = dot(source(kx, 0, first_r, n), qt)
            for k in range(n):
                r = first_r + k
                s = big[k * BLK:(k + 1) * BLK]
                if HALO <= r < BAND:
                    s = jnp.where(row_full <= lane_full - BLK * (r - HALO), s, NEG)
                st[slot, r * BLK:(r + 1) * BLK] = s
                here = jnp.max(s.reshape(BLK // 8, 8, 2 * BLK), axis=0)
                here = jnp.where(allowed(r), here, NEG)
                keep["top"] = jnp.maximum(keep["top"], here) if r else here

        def after_scores():
            keep["top"] = jnp.max(keep["top"], axis=0, keepdims=True) * c

        def weigh(first_r, n):
            for k in range(n):
                r = first_r + k
                off = jnp.where(allowed(r), keep["top"], -NEG)
                e = jnp.exp2(st[slot, r * BLK:(r + 1) * BLK] * c - off)
                probs(first_r, n)[k * BLK:(k + 1) * BLK] = e.astype(BF16)

        cols = pl.ds(pl.multiple_of(t0 * BLK, 2 * BLK), cut)

        def attend():
            ot = dot(vt[ch, :, cols], pb[tt])
            if wide:
                ot = ot + dot(vgt[:, :wide], pg[slot, :wide])
            keep["inv"] = inv = 1.0 / ot[HD:HD + 1]
            ot = ot[:HD] * inv
            ob = ot.astype(BF16)
            dof = dot_.astype(F32)
            keep["delta"] = jnp.sum(ob.astype(F32) * dof, axis=0, keepdims=True)
            odq[pl.ds(pos, 2), 0] = ob.T.reshape(2, BLK, HD)
            col = jnp.broadcast_to(inv, (8, 2 * BLK)).T[:, :1]
            qs[tt] = (q.astype(F32) * col).astype(BF16)
            dos[tt] = (do.astype(F32) * col).astype(BF16)

        def back(r, n):
            g = dot(source(vx, 1, r, n), dot_) - keep["delta"]
            grads(r, n)[...] = probs(r, n)[...] * g.astype(BF16)

        def finish_tile():
            dqt = dot(kt[ch, :, cols], ds[tt])
            if wide:
                dqt = dqt + dot(kgt[:, :wide], dg[slot, :wide])
            dqt = dqt * (keep["inv"] * SCALE)
            odq[pl.ds(pos, 2), 1] = dqt.astype(BF16).T.reshape(2, BLK, HD)

        return scores, after_scores, weigh, attend, back, finish_tile

    vt[:, HD:] = jnp.ones((2, ONES, EXT * BLK + BLK), BF16)
    vgt[HD:] = jnp.ones((ONES, GLOB * BLK), BF16)
    dkg[...] = jnp.zeros_like(dkg)
    dvg[...] = jnp.zeros_like(dvg)

    def group(ch, i, parts):
        wide = parts * BLK
        segs = [(r, UNIT) for r in range(0, BAND, UNIT)] + [(BAND + k, min(UNIT, parts - k)) for k in range(0, parts, UNIT)]
        stages = [tile(ch, 4 * i + k, k, wide) for k in range(4)]
        scores, after_scores, weigh, attend, back, finish_tile = zip(*stages)
        for seg in segs:
            for f in scores:
                f(*seg)
        for f in after_scores:
            f()
        for seg in segs:
            for f in weigh:
                f(*seg)
        for f in attend:
            f()
        for seg in segs:
            for f in back:
                f(*seg)
        for f in finish_tile:
            f()
        if parts:
            for weights, rows_of, total in ((dg, qs, dkg), (pg, dos, dvg)):
                acc = total[:wide]
                for k in range(4):
                    acc = acc + dot(weights[k, :wide], rows_of[4 * i + k])
                total[:wide] = acc

    def run(ch, outer):
        def step(i, carry):
            last = info[2 + ch] + 8 * i + 7
            count = (info[4] <= last - w).astype(jnp.int32)
            for g in range(1, GLOB):
                count += (info[4 + g] <= last - w).astype(jnp.int32)
            for least, parts in zip((-1,) + STEPS, STEPS):
                @pl.when(jnp.logical_and(count > least, count <= parts))
                def _(parts=parts):
                    group(ch, i, parts)
            return carry

        lax.fori_loop(0, RUN // 8, step, 0)

        for u in range((EXT + 1) // 2):
            for part, (weights, rows_of) in enumerate(((ds, qs), (pb, dos))):
                acc = [None, None]
                for tt in range(max(0, u - 4), min(RUN // 2, u + 1)):
                    r = 2 * (u - tt)
                    n = min(2, BAND - r)
                    if n == 2:
                        g = dot(weights[tt, r * BLK:(r + 2) * BLK], rows_of[tt])
                        g = [g[:BLK], g[BLK:]]
                    else:
                        g = [dot(weights[tt, r * BLK:(r + 1) * BLK], rows_of[tt])]
                    for k in range(n):
                        acc[k] = g[k] if acc[k] is None else acc[k] + g[k]
                for k in range(2):
                    e = 2 * u + k
                    if e >= EXT or acc[k] is None:
                        continue
                    g = acc[k] * SCALE if part == 0 else acc[k]
                    if e < HALO:
                        head[ch, e, part] = g
                    else:
                        t = e - HALO
                        own[jnp.where(ch == 0, place(0, t), place(1, t)), part] = g.astype(BF16)
                    if e >= RUN:
                        tail[ch, e - RUN, part] = g
        return outer

    lax.fori_loop(0, 2, run, 0)
    for h in range(HALO):
        back_a[h] = head[0, h].astype(BF16)
        back_b[h] = head[1, h].astype(BF16)

    @pl.when(last_y == 1)
    def _():
        for h in range(HALO):
            own[17 + h] = (tail[0, h] + head[1, h]).astype(BF16)

    for s in range(GLOB):
        glob_grad[s, 0] = (dkg[s * BLK:(s + 1) * BLK] * SCALE).astype(BF16)
        glob_grad[s, 1] = dvg[s * BLK:(s + 1) * BLK].astype(BF16)


def place(ch, t):
    return (t // 8) * 16 + t % 8 if ch == 0 else (1 - t // 8) * 16 + 8 + t % 8


def vmem():
    return pl.BlockSpec(memory_space=pltpu.VMEM)


def attention(info, kv, qd, halo_a, halo_b, glob):
    sds = jax.ShapeDtypeStruct
    return pl.pallas_call(
        attention_kernel,
        out_shape=(
            sds((32, 2, BLK, HD), BF16),
            sds((32, 2, BLK, HD), BF16),
            sds((HALO, 2, BLK, HD), BF16),
            sds((HALO, 2, BLK, HD), BF16),
            sds((GLOB, 2, BLK, HD), BF16),
        ),
        in_specs=[pl.BlockSpec(memory_space=pltpu.SMEM)] + [vmem()] * 5,
        out_specs=(vmem(),) * 5,
        scratch_shapes=[
            pltpu.VMEM((2, EXT, BLK, HD), BF16),
            pltpu.VMEM((2, EXT, BLK, HD), BF16),
            pltpu.VMEM((2, HD, EXT * BLK + BLK), BF16),
            pltpu.VMEM((2, HD + ONES, EXT * BLK + BLK), BF16),
            pltpu.VMEM((HD, GLOB * BLK), BF16),
            pltpu.VMEM((HD + ONES, GLOB * BLK), BF16),
            pltpu.VMEM((RUN // 2, 2 * BLK, HD), BF16),
            pltpu.VMEM((RUN // 2, 2 * BLK, HD), BF16),
            pltpu.VMEM((4, (BAND + GLOB) * BLK, 2 * BLK), F32),
            pltpu.VMEM((RUN // 2, BAND * BLK, 2 * BLK), BF16),
            pltpu.VMEM((RUN // 2, BAND * BLK, 2 * BLK), BF16),
            pltpu.VMEM((4, GLOB * BLK, 2 * BLK), BF16),
            pltpu.VMEM((4, GLOB * BLK, 2 * BLK), BF16),
            pltpu.VMEM((GLOB * BLK, HD), F32),
            pltpu.VMEM((GLOB * BLK, HD), F32),
            pltpu.VMEM((2, HALO, 2, BLK, HD), F32),
            pltpu.VMEM((2, HALO, 2, BLK, HD), F32),
        ],
        compiler_params=pltpu.CompilerParams(vmem_limit_bytes=52 * 2**20),
        cost_estimate=pl.CostEstimate(
            flops=12 * 448 * BLK**3, bytes_accessed=16 * 2**20, transcendentals=448 * BLK * BLK
        ),
        name="attention",
    )(info, kv, qd, halo_a, halo_b, glob)


def finish_kernel(info, own, back_a, back_b, glob_one, glob_two, out):
    for p in range(32):
        if 17 <= p < 24:
            out[p] = (own[p].astype(F32) + back_a[p - 17].astype(F32)).astype(BF16)
        elif 9 <= p < 16:
            out[p] = (own[p].astype(F32) + back_b[p - 9].astype(F32)).astype(BF16)
        else:
            out[p] = own[p]
    for s in range(GLOB):
        @pl.when(info[16 + s] == 1)
        def _(s=s):
            p = info[10 + s]
            ia = jnp.clip(p - 17, 0, HALO - 1)
            ib = jnp.clip(p - 9, 0, HALO - 1)
            in_a = jnp.logical_and(p >= 17, p < 24)
            in_b = jnp.logical_and(p >= 9, p < 16)
            g = own[p].astype(F32) + glob_one[s].astype(F32) + glob_two[s].astype(F32)
            g = g + jnp.where(in_a, back_a[ia].astype(F32), 0.0)
            g = g + jnp.where(in_b, back_b[ib].astype(F32), 0.0)
            out[p] = g.astype(BF16)


def finish(info, own, back_a, back_b, glob_one, glob_two):
    return pl.pallas_call(
        finish_kernel,
        out_shape=jax.ShapeDtypeStruct((32, 2, BLK, HD), BF16),
        in_specs=[pl.BlockSpec(memory_space=pltpu.SMEM)] + [vmem()] * 5,
        out_specs=vmem(),
        compiler_params=pltpu.CompilerParams(vmem_limit_bytes=16 * 2**20),
        cost_estimate=pl.CostEstimate(flops=2**21, bytes_accessed=6 * 2**20, transcendentals=0),
        name="finish",
    )(info, own, back_a, back_b, glob_one, glob_two)


def to_heads(x, y):
    pair = jnp.stack([x, y], axis=0).reshape(2, BLK, 16, 2, HD)
    pair = jnp.transpose(pair, (3, 2, 0, 1, 4)).reshape(32, 2, BLK, HD)
    return pair


def to_rows(pair):
    pair = pair.reshape(2, 16, 2, BLK, HD)
    pair = jnp.transpose(pair, (2, 3, 1, 0, 4)).reshape(2, BLK, 32, HD)
    return pair[0], pair[1]


def exchange(x):
    return lax.all_to_all(x, GROUP, 0, 0, tiled=True)


PAIR_ONE = [(0, 1), (1, 0), (2, 3), (3, 2)]
PAIR_TWO = [(1, 2), (2, 1), (3, 0), (0, 3)]


def shards(query, keys, values, grad_out, window, global_blocks):
    me = lax.axis_index("y")
    w = jnp.where(lax.axis_index("xh") == 0, window[0], window[1])
    before = global_blocks[None, :] < global_blocks[:, None]
    rank = jnp.sum(before.astype(jnp.int32), axis=1)
    chosen = rank[None, :] == jnp.arange(GLOB, dtype=jnp.int32)[:, None]
    global_blocks = jnp.sum(jnp.where(chosen, global_blocks[None, :], 0), axis=1)
    low = global_blocks < 64
    owner = jnp.where(low, global_blocks // RUN, (127 - global_blocks) // RUN)
    t = global_blocks % RUN
    where = jnp.where(low, (t // 8) * 16 + t % 8, (1 - t // 8) * 16 + 8 + t % 8)
    info = jnp.concatenate([
        jnp.stack([w, (me == 3).astype(jnp.int32), RUN * me, 112 - RUN * me]),
        global_blocks, where, (owner == me).astype(jnp.int32),
    ]).astype(jnp.int32)

    kv = exchange(to_heads(keys, values))
    qd = exchange(to_heads(query, grad_out))

    halo_a = lax.ppermute(kv[17:24], "y", [(0, 1), (1, 2), (2, 3)])
    halo_b = lax.ppermute(kv[9:16], "y", [(3, 2), (2, 1), (1, 0)])
    mine = jnp.concatenate([lax.dynamic_slice_in_dim(kv, where[s], 1, 0) for s in range(GLOB)], axis=0)
    other = lax.ppermute(mine, "y", PAIR_ONE)
    mine = jnp.where((owner == me)[:, None, None, None], mine, other)
    other = lax.ppermute(mine, "y", PAIR_TWO)
    glob = jnp.where((owner // 2 == me // 2)[:, None, None, None], mine, other)

    odq, own, back_a, back_b, glob_grad = attention(info, kv, qd, halo_a, halo_b, glob)

    odq = exchange(odq)
    back_a = lax.ppermute(back_a, "y", [(1, 0), (2, 1), (3, 2)])
    back_b = lax.ppermute(back_b, "y", [(0, 1), (1, 2), (2, 3)])
    other = lax.ppermute(glob_grad, "y", PAIR_ONE)
    glob_grad = (glob_grad.astype(F32) + other.astype(F32)).astype(BF16)
    other = lax.ppermute(glob_grad, "y", PAIR_TWO)
    dkv = exchange(finish(info, own, back_a, back_b, glob_grad, other))
    attended, grad_query = to_rows(odq)
    grad_keys, grad_values = to_rows(dkv)
    return attended, grad_query, grad_keys, grad_values


def solution(mesh):
    fine = Mesh(mesh.devices.reshape(4, 2, 2, 4, 2), ("y", "xh", "xl", "z", "c"))
    rows = P(("y", "xh", "xl", "z", "c"), None, None)
    return jax.shard_map(
        shards,
        mesh=fine,
        in_specs=(rows, rows, rows, rows, P(("xl", "z", "c")), P()),
        out_specs=(rows,) * 4,
        check_vma=False,
    )
```
